128 devices in a mesh: angle: 8 (over x, y_lo), row: 16 (over z, y_hi, core).
Axes of the slice: x: 4, y: 4 (y_hi: 2, y_lo: 2; y = y_hi * 2 + y_lo), z: 4, core: 2. Of those that a mesh axis runs over, the one named last changes fastest.
Arguments:
- hologram: bfloat16 [16, 2048, 2048], P('angle', 'row'), may hold values from -6 to 6
- centres: int32 [16, 2], P('angle'), may hold values from 256 to 767
- offsets: int32 [16, 16, 16], P('angle', 'row'), may hold values from -1 to 1
- angle_index: int32 [16], replicated, may hold values from 0 to 1199
Outputs:
- volume: float32 [8, 1024, 1024], P('angle', 'row')
The draws below stay inside these ranges and needn't reach their ends.
Inputs may be any that keep to these rules, and one draw needn't show every extreme that they name: `angle_index`: angle indices into the scan of 1200 angles.
All inputs are finite; a program needn't handle non-finite values.
Results may differ from the reference program's by a relative error of at most 0.02.
Values may be sent and summed in bfloat16 or wider, within the bound.
A program may use at most 192 MiB of HBM per device.

```python
import math
import jax
import jax.numpy as jnp
from jax import lax

PIX = 2048
CROP = 1024
BLOCK = 64
PLANES = 8
ANGLES = 1200
HOLOS = 16


def plant(values, key, least, largest):
    dims = values.shape
    spot = [jax.random.randint(jax.random.fold_in(key, axis), (), 0, dims[axis]) for axis in range(len(dims))]
    values = values.at[tuple(spot)].set(least)
    longest = dims.index(max(dims))
    spot[longest] = (spot[longest] + 1) % dims[longest]
    return values.at[tuple(spot)].set(largest)


def levels(stream_key, extent, shards, least, largest):
    gain = 1.0
    for dim, shards_of in shards:
        steps = jax.random.uniform(jax.random.fold_in(jax.random.fold_in(stream_key, 6), dim), (shards_of,), jnp.float32, least / len(shards), largest / len(shards))
        gain = gain * jnp.repeat(jnp.exp(steps), extent[dim] // shards_of).reshape((-1,) + (1,) * (len(extent) - 1 - dim))
    return gain


def centred(rng, extent, spread, reach, pieces=(), kind=jnp.bfloat16):
    drawn = jax.random.normal(rng, extent, jnp.float32) * spread
    if len(pieces) > 0:
        drawn = levels(rng, extent, pieces, -0.22, 0.18) * drawn
    return jnp.clip(drawn, min=-reach, max=reach).astype(kind)


def setup_inputs(seed: int = 0) -> dict:
    key_list = jax.random.split(jax.random.key(seed), 5)
    hologram = centred(key_list[0], (HOLOS, PIX, PIX), 1.0, 6.0, ((0, 8), (1, 16)))
    centres = plant(jax.random.randint(key_list[1], (HOLOS, 2), PIX // 8, 3 * PIX // 8), jax.random.fold_in(key_list[1], 1), PIX // 8, (3 * PIX // 8) - 1).astype(jnp.int32)
    offsets = plant(jax.random.randint(key_list[2], (HOLOS, CROP // BLOCK, CROP // BLOCK), -1, 2), jax.random.fold_in(key_list[2], 1), -1, 1).astype(jnp.int32)
    angle_index = plant(jax.random.randint(key_list[3], (HOLOS,), 0, ANGLES), jax.random.fold_in(key_list[3], 1), 0, ANGLES - 1).astype(jnp.int32)
    return {"hologram": hologram, "centres": centres, "offsets": offsets, "angle_index": angle_index}


full_turn = 2.0 * math.pi
wave_number = 4.0

def turn_table(left_ints, right_ints, period):
    product = jnp.mod(left_ints[:, None] * right_ints[None, :], period).astype(jnp.int32)
    angles = product.astype(jnp.float32) * jnp.float32(full_turn / period)
    factor = jnp.float32(1.0 / math.sqrt(period))
    return ((jnp.cos(angles) * factor).astype(jnp.bfloat16), (jnp.sin(angles) * factor).astype(jnp.bfloat16))

def angle_trig(angle_at):
    tilt_angle = angle_at.astype(jnp.float32) * jnp.float32(full_turn / ANGLES)
    return (jnp.cos(tilt_angle), jnp.sin(tilt_angle))

def plane_kernel(cosine, sine_value, depth_at, holo_count):
    shifted = jnp.arange(CROP, dtype=jnp.int32) - CROP // 2
    spatial = shifted.astype(jnp.float32) * jnp.float32(full_turn / CROP)
    lateral = shifted.astype(jnp.float32)
    along_axis = lateral * cosine + depth_at * sine_value
    depth_axis = depth_at * cosine - lateral * sine_value
    axial = jnp.sqrt(wave_number * wave_number - spatial * spatial) - wave_number
    phases = spatial[:, None] * along_axis[None, :] + axial[:, None] * depth_axis[None, :]
    weight = jnp.abs(spatial) / jnp.float32(math.pi * math.sqrt(CROP * holo_count))
    real_part = (weight[:, None] * jnp.cos(phases)).astype(jnp.bfloat16)
    imag_part = (weight[:, None] * jnp.sin(phases)).astype(jnp.bfloat16)
    return jnp.concatenate([real_part, imag_part], axis=0)

def mat(left, right):
    return jnp.dot(left, right, preferred_element_type=jnp.float32)

def hologram_field(picture, centre, offset):
    pixels = jnp.arange(PIX, dtype=jnp.int32)
    freq_bins = jnp.arange(CROP, dtype=jnp.int32)
    cols_cos, cols_sin = turn_table(pixels, centre[0] - CROP // 2 + freq_bins, PIX)
    row_spec = mat(picture, jnp.concatenate([cols_cos, -cols_sin], axis=1)).astype(jnp.bfloat16)
    row_real = row_spec[:, :CROP]
    row_imag = row_spec[:, CROP:]
    rows_cos, rows_sin = turn_table(pixels, centre[1] - CROP // 2 + freq_bins, PIX)
    spec_real = (mat(rows_cos.T, row_real) + mat(rows_sin.T, row_imag)).astype(jnp.bfloat16)
    spec_imag = (mat(rows_cos.T, row_imag) - mat(rows_sin.T, row_real)).astype(jnp.bfloat16)
    back_cos, back_sin = turn_table(freq_bins - CROP // 2, freq_bins, CROP)
    mid_real = (mat(back_cos.T, spec_real) - mat(back_sin.T, spec_imag)).astype(jnp.bfloat16)
    mid_imag = (mat(back_sin.T, spec_real) + mat(back_cos.T, spec_imag)).astype(jnp.bfloat16)
    field_real = mat(mid_real, back_cos) - mat(mid_imag, back_sin)
    field_imag = mat(mid_real, back_sin) + mat(mid_imag, back_cos)
    energy = field_real * field_real + field_imag * field_imag + 1.0
    magnitude = jnp.sqrt(energy)
    unwrap = jnp.repeat(jnp.repeat(offset, BLOCK, axis=0), BLOCK, axis=1).astype(jnp.float32)
    ry_real = (0.5 * jnp.log(energy)).astype(jnp.bfloat16)
    ry_imag = (2.0 * jnp.arctan(field_imag / (magnitude + jnp.abs(field_real))) + full_turn * unwrap).astype(jnp.bfloat16)
    wave_cos, wave_sin = turn_table(freq_bins - CROP // 2, freq_bins - CROP // 2, CROP)
    filt_real = (mat(ry_real, wave_cos) + mat(ry_imag, wave_sin)).astype(jnp.bfloat16)
    filt_imag = (mat(ry_imag, wave_cos) - mat(ry_real, wave_sin)).astype(jnp.bfloat16)
    return jnp.concatenate([filt_real, -filt_imag], axis=1)

def reference(hologram, centres, offsets, angle_index):
    holo_count = hologram.shape[0]

    def accumulate(running, inputs):
        picture, centre, offset, angle_at = inputs
        filtered = hologram_field(picture, centre, offset)
        cosine, sine_value = angle_trig(angle_at)
        slices_list = [mat(filtered, plane_kernel(cosine, sine_value, jnp.float32(plane_num - PLANES // 2), holo_count)) for plane_num in range(PLANES)]
        return (running + jnp.stack(slices_list), None)
    empty_sum = jnp.zeros((PLANES, CROP, CROP), jnp.float32)
    volume, _ = lax.scan(accumulate, empty_sum, (hologram, centres, offsets, angle_index))
    return volume
```

```python
import functools
import math

import jax
import jax.numpy as jnp
import numpy as np
from jax import lax
from jax.experimental import pallas as pl
from jax.experimental.pallas import tpu as pltpu
from jax.sharding import PartitionSpec as P

PIX = 2048
CROP = 1024
BLOCK = 64
PLANES = 8
ANGLES = 1200
HOLOS = 16

ROWS = 16
GROUPS = 8
HELD = HOLOS // GROUPS
SLAB = CROP // ROWS
LANE = 128
WIDE = 256
SLABS = CROP // LANE

MESH = pl.DeviceIdType.MESH
f32 = jnp.float32
bf16 = jnp.bfloat16

SIN = (6.283185302511503, -41.34170040531721, 81.6051313857832, -76.70301535364747, 42.02592698447418,
       -14.899846663536497, 3.2381375046186873)
COS = (0.9999999890590228, -19.73920449945383, 64.93911745989081, -85.45013953079767, 60.167630950263465,
       -25.967599245923743, 6.52865815775625)
ATAN = (0.9999999842426363, -0.33333066780691484, 0.19992483578502865, -0.14202570511730603, 0.10636754098309847,
        -0.07495445443851168, 0.04258760747298536, -0.016005030509000328, 0.002834064300549813)


def poly(coefs, v):
    total = jnp.full_like(v, coefs[-1])
    for coef in coefs[-2::-1]:
        total = total * v + f32(coef)
    return total


def turns(x):
    u = x - jnp.round(x)
    v = u * u
    return poly(COS, v), u * poly(SIN, v)


def half_band(n):
    n = n.astype(np.float64)
    with np.errstate(all="ignore"):
        odd = np.sin(np.pi * n / 2) / np.sin(np.pi * n / PIX) / CROP
    return np.where(n == 0, 1.0, np.where(n % 2 == 0, 0.0, odd))


def half_band_strips():
    x = np.arange(PIX + 3 * 512)[:, None] - 3 * 512
    b = np.arange(WIDE)
    along_x = half_band(2 * b[None, :] - x)
    i = np.arange(CROP + 3 * WIDE)[None, :] - 3 * WIDE
    along_y = half_band(2 * (b[:, None] - i) - 1)
    return along_x.astype(bf16), along_y.astype(bf16)


def iota(shape, dim):
    return lax.broadcasted_iota(jnp.int32, shape, dim)


def dot(a, b):
    return jnp.dot(a, b, preferred_element_type=f32)


def kernel(centres, angle_index, offsets, hologram, x_hbm, y_hbm, out,
           x_strip, y_strip, q_tab, p_tab, lhs, even, send1, recv1, send2, recv2, rot, ryt, wave, back, plane_tab,
           spread, acc, own, send3, recv3, copy_sem, s1, r1, s2, r2, s3, r3):
    row = lax.axis_index("row")
    group = lax.axis_index("angle")

    x_copy = pltpu.make_async_copy(x_hbm, x_strip, copy_sem.at[0])
    y_copy = pltpu.make_async_copy(y_hbm, y_strip, copy_sem.at[1])
    x_copy.start()
    y_copy.start()

    barrier = pltpu.get_barrier_semaphore()

    def greet_row(i, carry):
        pl.semaphore_signal(barrier, inc=1, device_id={"row": lax.rem(row + i, ROWS)}, device_id_type=MESH)
        return carry

    def greet_group(i, carry):
        pl.semaphore_signal(barrier, inc=1, device_id={"angle": lax.rem(group + i, GROUPS)}, device_id_type=MESH)
        return carry

    lax.fori_loop(1, ROWS, greet_row, 0)
    lax.fori_loop(1, GROUPS, greet_group, 0)

    at_x = LANE * iota((PIX // LANE, LANE), 0) + iota((PIX // LANE, LANE), 1)
    for h in range(HELD):
        m = (at_x * (2 * centres[h, 0] - 1)) & (2 * PIX - 1)
        c, s = turns(m.astype(f32) * f32(1.0 / (2 * PIX)))
        q_tab[2 * h] = c
        q_tab[2 * h + 1] = -s
    at_y = 2 * SLAB * row + 2 * iota((SLAB, LANE), 0)
    for parity in range(2):
        for h in range(HELD):
            m = ((at_y + (1 - parity)) * (2 * centres[h, 1] - 1)) & (2 * PIX - 1)
            c, s = turns(m.astype(f32) * f32(1.0 / (2 * PIX)))
            p_tab[4 * parity + 2 * h] = 0.5 * c
            p_tab[4 * parity + 2 * h + 1] = -0.5 * s

    wanted = iota((2 * SLAB, 2 * SLAB), 0)
    wanted = jnp.where(wanted < SLAB, 2 * wanted + 1, 2 * wanted - 2 * SLAB)
    sort_rows = jnp.where(wanted == iota((2 * SLAB, 2 * SLAB), 1), 1.0, 0.0).astype(bf16)

    def modulate(k, carry):
        at = pl.multiple_of(WIDE * k, WIDE)
        for h in range(HELD):
            sorted_rows = dot(sort_rows, hologram[h, :, pl.ds(at, WIDE)])
            for part in range(2):
                for side in range(2):
                    phase = q_tab[2 * h + part, pl.ds(2 * k + side, 1), :]
                    for parity in range(2):
                        block = sorted_rows[parity * SLAB:(parity + 1) * SLAB, side * LANE:(side + 1) * LANE]
                        first = 4 * SLAB * parity + 2 * SLAB * h + SLAB * part
                        lhs[first:first + SLAB, pl.ds(pl.multiple_of(at + side * LANE, LANE), LANE)] = (
                            block * phase
                        ).astype(bf16)
        return carry

    lax.fori_loop(0, PIX // WIDE, modulate, 0)
    x_copy.wait()

    def across(parity, block):
        weights = x_strip[pl.ds(pl.multiple_of(3 * 512 - 512 * block, 512), PIX), :]
        z = dot(lhs[4 * SLAB * parity:4 * SLAB * (parity + 1), :], weights)
        for h in range(HELD):
            c = p_tab[4 * parity + 2 * h]
            s = p_tab[4 * parity + 2 * h + 1]
            for side in range(2):
                re = z[2 * SLAB * h:2 * SLAB * h + SLAB, side * LANE:(side + 1) * LANE]
                im = z[2 * SLAB * h + SLAB:2 * SLAB * (h + 1), side * LANE:(side + 1) * LANE]
                yield h, side, re * c - im * s, re * s + im * c

    def to_row(send, recv, sends, recvs, to):
        return pltpu.make_async_remote_copy(
            src_ref=send.at[to], dst_ref=recv.at[row], send_sem=sends.at[to], recv_sem=recvs.at[row],
            device_id={"row": to}, device_id_type=MESH)

    def from_row(send, recv, sends, recvs, source):
        return pltpu.make_async_remote_copy(
            src_ref=send.at[source], dst_ref=recv.at[source], send_sem=sends.at[source], recv_sem=recvs.at[source],
            device_id={"row": source}, device_id_type=MESH)

    pl.semaphore_wait(barrier, ROWS + GROUPS - 2)

    def odd_rows(k, carry):
        block = lax.rem(row + k, 4)
        for h, side, re, im in across(0, block):
            to = SLABS * h + 2 * block + side
            send1[to, :, 0:LANE] = re.astype(bf16)
            send1[to, :, LANE:WIDE] = im.astype(bf16)

            @pl.when(to != row)
            def _():
                to_row(send1, recv1, s1, r1, to).start()

            @pl.when(to == row)
            def _():
                recv1[row] = send1[row]
        return carry

    lax.fori_loop(0, 4, odd_rows, 0)

    def even_rows(block, carry):
        for h, side, re, im in across(1, block):
            at = pl.ds(pl.multiple_of(WIDE * block + LANE * side, LANE), LANE)
            even[2 * h, :, at] = re
            even[2 * h + 1, :, at] = im
        return carry

    lax.fori_loop(0, 4, even_rows, 0)

    def table(freq, store):
        chunk = 16
        lanes = iota((chunk, LANE), 1).astype(f32)

        def rows_of(k, carry):
            at = pl.multiple_of(chunk * k, chunk)
            j = (iota((chunk, LANE), 0) + (chunk * k - CROP // 2)).astype(f32)
            alpha = freq(j)
            c0, s0 = turns(alpha * lanes)
            cr, sr = turns(alpha * f32(LANE))
            c, s = c0, s0
            for a in range(4):
                store(at, a + 4, c, -s)
                if a < 3:
                    c, s = c * cr - s * sr, s * cr + c * sr
            c, s = c0, s0
            for a in range(3, -1, -1):
                c, s = c * cr + s * sr, s * cr - c * sr
                store(at, a, c, -s)
            return carry

        lax.fori_loop(0, CROP // chunk, rows_of, 0)

    def wave_store(at, a, c, s):
        wave[pl.ds(at, 16), a * LANE:(a + 1) * LANE] = c.astype(bf16)
        wave[pl.ds(at, 16), CROP + a * LANE:CROP + (a + 1) * LANE] = s.astype(bf16)

    table(lambda j: j * f32(1.0 / CROP), wave_store)

    def tilt(h, shape):
        index = jnp.full(shape, angle_index[HELD * group + h], jnp.int32)
        return turns(index.astype(f32) * f32(1.0 / ANGLES))

    def axial(spatial):
        turn = spatial * f32(2.0 * math.pi)
        return (jnp.sqrt(16.0 - turn * turn) - 4.0) * f32(0.5 / math.pi)

    def back_table(h):
        c, s = tilt(h, (16, LANE))

        def freq(j):
            spatial = j * f32(1.0 / CROP)
            return spatial * c - axial(spatial) * s

        def store(at, a, c, s):
            back[pl.ds(2 * h * CROP + at, 16), a * LANE:(a + 1) * LANE] = c.astype(bf16)
            back[pl.ds((2 * h + 1) * CROP + at, 16), a * LANE:(a + 1) * LANE] = s.astype(bf16)

        table(freq, store)

    back_table(0)

    y_copy.wait()

    def wait_first(i, carry):
        from_row(send1, recv1, s1, r1, lax.rem(row + i, ROWS)).wait_recv()
        return carry

    lax.fori_loop(1, ROWS, wait_first, 0)
    gathered = recv1[...].reshape(CROP, WIDE)

    def down(k, carry):
        block = lax.rem(row // 4 + k, 4)
        weights = y_strip[:, pl.ds(pl.multiple_of(3 * WIDE - WIDE * block, WIDE), CROP)]
        z = dot(weights, gathered).astype(bf16)
        for part in range(4):
            to = 4 * block + part
            send2[to] = z[SLAB * part:SLAB * (part + 1), :]

            @pl.when(to != row)
            def _():
                to_row(send2, recv2, s2, r2, to).start()

            @pl.when(to == row)
            def _():
                recv2[row] = send2[row]
        return carry

    lax.fori_loop(0, 4, down, 0)

    back_table(1)

    spatial = (LANE * iota((SLABS, LANE), 0) + iota((SLABS, LANE), 1) - CROP // 2).astype(f32) * f32(1.0 / CROP)
    ramp = jnp.abs(spatial) * f32(2.0 / math.sqrt(CROP * HOLOS) / math.sqrt(CROP))
    for h in range(HELD):
        c, s = tilt(h, (SLABS, LANE))
        beta = spatial * s + axial(spatial) * c
        for d in range(PLANES):
            pc, ps = turns(beta * f32(d - PLANES // 2))
            plane_tab[2 * (PLANES * h + d)] = pc * ramp
            plane_tab[2 * (PLANES * h + d) + 1] = ps * ramp

    def rotations(k, carry):
        at = LANE * k
        m = (iota((SLAB, LANE), 1) + at + iota((SLAB, LANE), 0) + SLAB * row).astype(f32)
        c, s = turns(m * f32(0.5 / CROP))
        lanes = pl.ds(pl.multiple_of(at, LANE), LANE)
        rot[0, :, lanes] = c
        rot[1, :, lanes] = -s
        return carry

    lax.fori_loop(0, SLABS, rotations, 0)

    left_half = iota((SLAB, LANE), 1) < BLOCK

    def rytov(i, carry):
        source = lax.rem(row + i, ROWS)

        @pl.when(i > 0)
        def _():
            from_row(send2, recv2, s2, r2, source).wait_recv()

        h = source // SLABS
        slab = lax.rem(source, SLABS)
        lanes = pl.ds(pl.multiple_of(LANE * slab, LANE), LANE)
        re = even[2 * h, :, lanes] + recv2[source, :, 0:LANE].astype(f32)
        im = even[2 * h + 1, :, lanes] + recv2[source, :, LANE:WIDE].astype(f32)
        c = rot[0, :, lanes]
        s = rot[1, :, lanes]
        field_re = re * c - im * s
        field_im = re * s + im * c
        energy = field_re * field_re + field_im * field_im + 1.0
        t = field_im / (jnp.sqrt(energy) + jnp.abs(field_re))
        unwrap = jnp.where(left_half, offsets[h, 0, 2 * slab], offsets[h, 0, 2 * slab + 1]).astype(f32)
        turned = 2.0 * (t * poly(ATAN, t * t)) + f32(2.0 * math.pi) * unwrap
        at = pl.multiple_of(2 * SLAB * h, 2 * SLAB)
        ryt[pl.ds(at, SLAB), lanes] = (0.5 * jnp.log(energy)).astype(bf16)
        ryt[pl.ds(pl.multiple_of(at + SLAB, SLAB), SLAB), lanes] = turned.astype(bf16)
        return carry

    lax.fori_loop(0, ROWS, rytov, 0)

    def filtered(k, carry):
        at = pl.multiple_of(WIDE * k, WIDE)
        fc = dot(ryt[...], wave[:, pl.ds(at, WIDE)])
        fs = dot(ryt[...], wave[:, pl.ds(pl.multiple_of(CROP + at, WIDE), WIDE)])
        for h in range(HELD):
            top = slice(2 * SLAB * h, 2 * SLAB * h + SLAB)
            low = slice(2 * SLAB * h + SLAB, 2 * SLAB * (h + 1))
            re = fc[top] - fs[low]
            im = fc[low] + fs[top]
            for side in range(2):
                lanes = slice(side * LANE, (side + 1) * LANE)
                re_side, im_side = re[:, lanes], im[:, lanes]
                real_at = pl.ds(pl.multiple_of(2 * CROP * h + at + side * LANE, LANE), LANE)
                imag_at = pl.ds(pl.multiple_of(2 * CROP * h + CROP + at + side * LANE, LANE), LANE)
                for d in range(PLANES):
                    pc = plane_tab[2 * (PLANES * h + d), pl.ds(2 * k + side, 1), :]
                    ps = plane_tab[2 * (PLANES * h + d) + 1, pl.ds(2 * k + side, 1), :]
                    spread[d * SLAB:(d + 1) * SLAB, real_at] = (re_side * pc - im_side * ps).astype(bf16)
                    spread[d * SLAB:(d + 1) * SLAB, imag_at] = (re_side * ps + im_side * pc).astype(bf16)
        return carry

    lax.fori_loop(0, CROP // WIDE, filtered, 0)

    def to_group(k, to):
        return pltpu.make_async_remote_copy(
            src_ref=send3.at[k, to], dst_ref=recv3.at[k, group], send_sem=s3.at[k, to], recv_sem=r3.at[k, group],
            device_id={"angle": to}, device_id_type=MESH)

    def from_group(k, source):
        return pltpu.make_async_remote_copy(
            src_ref=send3.at[k, source], dst_ref=recv3.at[k, source], send_sem=s3.at[k, source],
            recv_sem=r3.at[k, source], device_id={"angle": source}, device_id_type=MESH)

    def planes(k, carry):
        at = pl.multiple_of(WIDE * k, WIDE)
        acc[...] = dot(spread[...], back[:, pl.ds(at, WIDE)])
        own[:, pl.ds(at, WIDE)] = acc[pl.ds(pl.multiple_of(SLAB * group, SLAB), SLAB), :]
        for d in range(PLANES):
            send3[k, d] = acc[d * SLAB:(d + 1) * SLAB, :].astype(bf16)

        def push(j, carry):
            to_group(k, lax.rem(group + j, GROUPS)).start()
            return carry

        lax.fori_loop(1, GROUPS, push, 0)
        return carry

    lax.fori_loop(0, CROP // WIDE, planes, 0)

    def collect(k, carry):
        at = pl.multiple_of(WIDE * k, WIDE)

        def take(j, total):
            source = lax.rem(group + j, GROUPS)
            from_group(k, source).wait_recv()
            return total + recv3[k, source].astype(f32)

        out[0, :, pl.ds(at, WIDE)] = lax.fori_loop(1, GROUPS, take, own[:, pl.ds(at, WIDE)])
        return carry

    lax.fori_loop(0, CROP // WIDE, collect, 0)

    def sent_row(i, carry):
        to = lax.rem(row + i, ROWS)
        to_row(send1, recv1, s1, r1, to).wait_send()
        to_row(send2, recv2, s2, r2, to).wait_send()
        return carry

    lax.fori_loop(1, ROWS, sent_row, 0)

    def sent_group(i, carry):
        to = lax.rem(group + lax.rem(i, GROUPS - 1) + 1, GROUPS)
        to_group(i // (GROUPS - 1), to).wait_send()
        return carry

    lax.fori_loop(0, (GROUPS - 1) * (CROP // WIDE), sent_group, 0)


def per_device(x_strip, y_strip, hologram, centres, offsets, angle_index):
    smem = pl.BlockSpec(memory_space=pltpu.SMEM)
    vmem = pl.BlockSpec(memory_space=pltpu.VMEM)
    anywhere = pl.BlockSpec(memory_space=pl.ANY)
    tiles = CROP // WIDE
    return pl.pallas_call(
        kernel,
        out_shape=jax.ShapeDtypeStruct((1, SLAB, CROP), f32),
        in_specs=[smem, smem, smem, vmem, anywhere, anywhere],
        out_specs=vmem,
        scratch_shapes=[
            pltpu.VMEM(x_strip.shape, bf16),
            pltpu.VMEM(y_strip.shape, bf16),
            pltpu.VMEM((2 * HELD, PIX // LANE, LANE), f32),
            pltpu.VMEM((4 * HELD, SLAB, LANE), f32),
            pltpu.VMEM((4 * HELD * SLAB, PIX), bf16),
            pltpu.VMEM((2 * HELD, SLAB, CROP), f32),
            pltpu.VMEM((ROWS, SLAB, WIDE), bf16),
            pltpu.VMEM((ROWS, SLAB, WIDE), bf16),
            pltpu.VMEM((ROWS, SLAB, WIDE), bf16),
            pltpu.VMEM((ROWS, SLAB, WIDE), bf16),
            pltpu.VMEM((2, SLAB, CROP), f32),
            pltpu.VMEM((2 * HELD * SLAB, CROP), bf16),
            pltpu.VMEM((CROP, 2 * CROP), bf16),
            pltpu.VMEM((2 * HELD * CROP, CROP), bf16),
            pltpu.VMEM((2 * HELD * PLANES, SLABS, LANE), f32),
            pltpu.VMEM((PLANES * SLAB, 2 * HELD * CROP), bf16),
            pltpu.VMEM((PLANES * SLAB, WIDE), f32),
            pltpu.VMEM((SLAB, CROP), f32),
            pltpu.VMEM((tiles, GROUPS, SLAB, WIDE), bf16),
            pltpu.VMEM((tiles, GROUPS, SLAB, WIDE), bf16),
            pltpu.SemaphoreType.DMA((2,)),
            pltpu.SemaphoreType.DMA((ROWS,)),
            pltpu.SemaphoreType.DMA((ROWS,)),
            pltpu.SemaphoreType.DMA((ROWS,)),
            pltpu.SemaphoreType.DMA((ROWS,)),
            pltpu.SemaphoreType.DMA((tiles, GROUPS)),
            pltpu.SemaphoreType.DMA((tiles, GROUPS)),
        ],
        compiler_params=pltpu.CompilerParams(
            collective_id=0, has_side_effects=True, vmem_limit_bytes=56 * 1024 * 1024
        ),
    )(centres, angle_index, offsets, hologram, x_strip, y_strip)


def solution(mesh):
    x_strip, y_strip = half_band_strips()
    placed = (P("angle", "row", None), P("angle", None), P("angle", "row", None), P())
    return jax.shard_map(
        functools.partial(per_device, x_strip, y_strip),
        mesh=mesh, in_specs=placed, out_specs=P("angle", "row", None), check_vma=False
    )
```

```python
import functools
import math

import jax
import jax.numpy as jnp
import numpy as np
from jax import lax
from jax.experimental import pallas as pl
from jax.experimental.pallas import tpu as pltpu
from jax.sharding import PartitionSpec as P

PIX = 2048
CROP = 1024
BLOCK = 64
PLANES = 8
ANGLES = 1200
HOLOS = 16

ROWS = 16
GROUPS = 8
HELD = HOLOS // GROUPS
SLAB = CROP // ROWS
LANE = 128
WIDE = 256
SLABS = CROP // LANE
HALVES = 2
HALF = SLAB // HALVES
TILE = 512
TILES = CROP // TILE

MESH = pl.DeviceIdType.MESH
f32 = jnp.float32
bf16 = jnp.bfloat16

SIN = (6.283185302511503, -41.34170040531721, 81.6051313857832, -76.70301535364747, 42.02592698447418,
       -14.899846663536497, 3.2381375046186873)
COS = (0.9999999890590228, -19.73920449945383, 64.93911745989081, -85.45013953079767, 60.167630950263465,
       -25.967599245923743, 6.52865815775625)
ATAN = (0.9999999842426363, -0.33333066780691484, 0.19992483578502865, -0.14202570511730603, 0.10636754098309847,
        -0.07495445443851168, 0.04258760747298536, -0.016005030509000328, 0.002834064300549813)


def poly(coefs, v):
    total = jnp.full_like(v, coefs[-1])
    for coef in coefs[-2::-1]:
        total = total * v + f32(coef)
    return total


def turns(x):
    u = x - jnp.round(x)
    v = u * u
    return poly(COS, v), u * poly(SIN, v)


def half_band(n):
    n = n.astype(np.float64)
    with np.errstate(all="ignore"):
        odd = np.sin(np.pi * n / 2) / np.sin(np.pi * n / PIX) / CROP
    return np.where(n == 0, 1.0, np.where(n % 2 == 0, 0.0, odd))


def half_band_strips():
    x = np.arange(PIX + 3 * 512)[:, None] - 3 * 512
    b = np.arange(WIDE)
    along_x = half_band(2 * b[None, :] - x)
    i = np.arange(CROP + 3 * WIDE)[None, :] - 3 * WIDE
    b = b.reshape(4, HALVES, HALF).transpose(1, 0, 2).reshape(WIDE)
    along_y = half_band(2 * (b[:, None] - i) - 1)
    return along_x.astype(bf16), along_y.astype(bf16)


def iota(shape, dim):
    return lax.broadcasted_iota(jnp.int32, shape, dim)


def dot(a, b):
    return jnp.dot(a, b, preferred_element_type=f32)


def dot_t(a, b):
    return lax.dot_general(a, b, (((1,), (1,)), ((), ())), preferred_element_type=f32)


def kernel(centres, angle_index, offsets, hologram, x_hbm, y_hbm, out,
           x_strip, y_strip, raw, q_tab, p_tab, odd, evens, even, send1, recv1, send2, recv2, rot, ryt, wave, back,
           turn_tab, plane_tab, spread, own, send3, recv3, copy_sem, s1, r1, s2, r2, s3, r3):
    row = lax.axis_index("row")
    group = lax.axis_index("angle")

    x_copy = pltpu.make_async_copy(x_hbm, x_strip, copy_sem.at[0])
    y_copy = pltpu.make_async_copy(y_hbm, y_strip, copy_sem.at[1])
    x_copy.start()
    y_copy.start()

    barrier = pltpu.get_barrier_semaphore()

    def greet_row(i, carry):
        pl.semaphore_signal(barrier, inc=1, device_id={"row": lax.rem(row + i, ROWS)}, device_id_type=MESH)
        return carry

    def greet_group(i, carry):
        pl.semaphore_signal(barrier, inc=1, device_id={"angle": lax.rem(group + i, GROUPS)}, device_id_type=MESH)
        return carry

    lax.fori_loop(1, ROWS, greet_row, 0)
    lax.fori_loop(1, GROUPS, greet_group, 0)

    at_x = LANE * iota((PIX // LANE, LANE), 0) + iota((PIX // LANE, LANE), 1)
    for h in range(HELD):
        m = (at_x * (2 * centres[h, 0] - 1)) & (2 * PIX - 1)
        c, s = turns(m.astype(f32) * f32(1.0 / (2 * PIX)))
        q_tab[2 * h] = c
        q_tab[2 * h + 1] = -s
    at_y = 2 * SLAB * row + 2 * iota((SLAB, LANE), 0)

    def row_phases(parity):
        for h in range(HELD):
            m = ((at_y + (1 - parity)) * (2 * centres[h, 1] - 1)) & (2 * PIX - 1)
            c, s = turns(m.astype(f32) * f32(1.0 / (2 * PIX)))
            p_tab[2 * h] = 0.5 * c
            p_tab[2 * h + 1] = -0.5 * s

    def modulate(parity, to):
        for a in range(PIX // LANE):
            lanes = slice(a * LANE, (a + 1) * LANE)
            for h in range(HELD):
                if parity == 0:
                    raw[h, a] = hologram[h, :, lanes].astype(f32)
                block = raw[h, a, pl.ds(1 - parity, SLAB, stride=2), :]
                for part in range(2):
                    first = 2 * SLAB * h + SLAB * part
                    to[first:first + SLAB, lanes] = (block * q_tab[2 * h + part, a:a + 1, :]).astype(bf16)

    def across(source, block):
        weights = x_strip[pl.ds(pl.multiple_of(3 * 512 - 512 * block, 512), PIX), :]
        z = dot(source[...], weights)
        for h in range(HELD):
            for side in range(2):
                c = p_tab[2 * h]
                s = p_tab[2 * h + 1]
                re = z[2 * SLAB * h:2 * SLAB * h + SLAB, side * LANE:(side + 1) * LANE]
                im = z[2 * SLAB * h + SLAB:2 * SLAB * (h + 1), side * LANE:(side + 1) * LANE]
                yield h, side, re * c - im * s, re * s + im * c

    modulate(0, odd)
    row_phases(0)
    x_copy.wait()
    pl.semaphore_wait(barrier, ROWS + GROUPS - 2)

    def first_copy(to):
        return pltpu.make_async_remote_copy(
            src_ref=send1.at[to], dst_ref=recv1.at[row], send_sem=s1.at[0], recv_sem=r1.at[0],
            device_id={"row": to}, device_id_type=MESH)

    def odd_rows(k, carry):
        pair = lax.rem(row // 4 + k, 2)
        for half in range(2):
            block = 2 * pair + half
            for h, side, re, im in across(odd, block):
                to = SLABS * h + 2 * block + side
                send1[to, :, 0:LANE] = re.astype(bf16)
                send1[to, :, LANE:WIDE] = im.astype(bf16)

        def push(i, carry):
            to = SLABS * (i // 4) + 4 * pair + lax.rem(row + i, 4)

            @pl.when(to != row)
            def _():
                first_copy(to).start()

            @pl.when(to == row)
            def _():
                recv1[row] = send1[row]
            return carry

        lax.fori_loop(0, 8, push, 0)
        return carry

    lax.fori_loop(0, 2, odd_rows, 0)

    def even_rows():
        modulate(1, evens)
        row_phases(1)
        for block in range(4):
            for h, side, re, im in across(evens, block):
                lanes = slice(WIDE * block + LANE * side, WIDE * block + LANE * (side + 1))
                even[2 * h, :, lanes] = re
                even[2 * h + 1, :, lanes] = im

    even_rows()

    def table(freq, target, cos_at):
        step = 16
        fine = iota((step, LANE), 0).astype(f32)
        coarse = ((iota((CROP // step, LANE), 0) - CROP // step // 2) * step).astype(f32)

        def columns(k, carry):
            def along(shape):
                return freq((iota(shape, 1) + (LANE * k - CROP // 2)).astype(f32))

            c0, s0 = turns(along((step, LANE)) * fine)
            c1, s1 = turns(along((CROP // step, LANE)) * coarse)
            turn_tab[0] = c1
            turn_tab[1] = s1
            cos_lanes = pl.ds(pl.multiple_of(cos_at + LANE * k, LANE), LANE)
            sin_lanes = pl.ds(pl.multiple_of(cos_at + CROP + LANE * k, LANE), LANE)
            for a in range(CROP // step):
                c = turn_tab[0, a:a + 1, :]
                s = turn_tab[1, a:a + 1, :]
                target[a * step:(a + 1) * step, cos_lanes] = (c0 * c - s0 * s).astype(bf16)
                target[a * step:(a + 1) * step, sin_lanes] = -(s0 * c + c0 * s).astype(bf16)
            return carry

        lax.fori_loop(0, SLABS, columns, 0)

    def tilt(h, shape):
        index = jnp.full(shape, angle_index[HELD * group + h], jnp.int32)
        return turns(index.astype(f32) * f32(1.0 / ANGLES))

    def axial(spatial):
        turn = spatial * f32(2.0 * math.pi)
        return (jnp.sqrt(16.0 - turn * turn) - 4.0) * f32(0.5 / math.pi)

    def back_table(h):
        def freq(j):
            c, s = tilt(h, j.shape)
            spatial = j * f32(1.0 / CROP)
            return spatial * c - axial(spatial) * s

        table(freq, back, 2 * h * CROP)

    table(lambda j: j * f32(1.0 / CROP), wave, 0)

    y_copy.wait()
    pltpu.make_async_remote_copy(
        src_ref=send1.at[0:ROWS - 1], dst_ref=recv1.at[0:ROWS - 1], send_sem=s1.at[0], recv_sem=r1.at[0],
        device_id={"row": row}, device_id_type=MESH).wait_recv()

    def second_copy(half, to):
        return pltpu.make_async_remote_copy(
            src_ref=send2.at[half, to], dst_ref=recv2.at[half, row], send_sem=s2.at[half], recv_sem=r2.at[half],
            device_id={"row": to}, device_id_type=MESH)

    def second_all(half):
        return pltpu.make_async_remote_copy(
            src_ref=send2.at[half, 0:ROWS - 1], dst_ref=recv2.at[half, 0:ROWS - 1], send_sem=s2.at[half],
            recv_sem=r2.at[half], device_id={"row": row}, device_id_type=MESH)

    gathered = recv1[...].reshape(CROP, WIDE)
    for half in range(HALVES):
        for block in range(4):
            first = 3 * WIDE - WIDE * block
            z = dot(y_strip[half * 4 * HALF:(half + 1) * 4 * HALF, first:first + CROP], gathered).astype(bf16)
            for part in range(4):
                send2[half, 4 * block + part] = z[HALF * part:HALF * (part + 1), :]

        def push(i, carry):
            second_copy(half, lax.rem(row + i, ROWS)).start()
            return carry

        lax.fori_loop(1, ROWS, push, 0)
        recv2[half, row] = send2[half, row]

    back_table(0)
    back_table(1)

    spatial = (LANE * iota((SLABS, LANE), 0) + iota((SLABS, LANE), 1) - CROP // 2).astype(f32) * f32(1.0 / CROP)
    ramp = jnp.abs(spatial) * f32(2.0 / math.sqrt(CROP * HOLOS) / math.sqrt(CROP))
    for h in range(HELD):
        c, s = tilt(h, (SLABS, LANE))
        beta = spatial * s + axial(spatial) * c
        for z in range(PLANES // 2 + 1):
            pc, ps = turns(beta * f32(z))
            plane_tab[h, z, 0] = pc * ramp
            plane_tab[h, z, 1] = ps * ramp

    def rotations(k, carry):
        at = LANE * k
        m = (iota((SLAB, LANE), 1) + at + iota((SLAB, LANE), 0) + SLAB * row).astype(f32)
        c, s = turns(m * f32(0.5 / CROP))
        lanes = pl.ds(pl.multiple_of(at, LANE), LANE)
        rot[0, :, lanes] = c
        rot[1, :, lanes] = -s
        return carry

    lax.fori_loop(0, SLABS, rotations, 0)

    left_half = iota((HALF, LANE), 1) < BLOCK

    def rytov(half):
        rows = slice(half * HALF, (half + 1) * HALF)

        def slab_of(slab, carry):
            lanes = pl.ds(pl.multiple_of(LANE * slab, LANE), LANE)
            c = rot[0, rows, lanes]
            s = rot[1, rows, lanes]
            for h in range(HELD):
                re = even[2 * h, rows, lanes] + recv2[half, SLABS * h + slab, :, 0:LANE].astype(f32)
                im = even[2 * h + 1, rows, lanes] + recv2[half, SLABS * h + slab, :, LANE:WIDE].astype(f32)
                field_re = re * c - im * s
                field_im = re * s + im * c
                energy = field_re * field_re + field_im * field_im + 1.0
                t = field_im / (jnp.sqrt(energy) + jnp.abs(field_re))
                unwrap = jnp.where(left_half, offsets[h, 0, 2 * slab], offsets[h, 0, 2 * slab + 1]).astype(f32)
                turned = 2.0 * (t * poly(ATAN, t * t)) + f32(2.0 * math.pi) * unwrap
                at = 2 * HALF * h
                ryt[half, at:at + HALF, lanes] = (0.5 * jnp.log(energy)).astype(bf16)
                ryt[half, at + HALF:at + 2 * HALF, lanes] = turned.astype(bf16)
            return carry

        lax.fori_loop(0, SLABS, slab_of, 0)

    def filtered(half):
        for k in range(CROP // WIDE):
            at = WIDE * k
            fc = dot(ryt[half], wave[:, at:at + WIDE])
            fs = dot(ryt[half], wave[:, CROP + at:CROP + at + WIDE])
            for h in range(HELD):
                top = slice(2 * HALF * h, 2 * HALF * h + HALF)
                low = slice(2 * HALF * h + HALF, 2 * HALF * (h + 1))
                for side in range(2):
                    lanes = slice(side * LANE, (side + 1) * LANE)
                    re = fc[top, lanes] - fs[low, lanes]
                    im = fc[low, lanes] + fs[top, lanes]
                    cos_at = 2 * CROP * h + at + side * LANE
                    sin_at = cos_at + CROP

                    def put(d, real, imag):
                        spread[half, d * HALF:(d + 1) * HALF, cos_at:cos_at + LANE] = real.astype(bf16)
                        spread[half, d * HALF:(d + 1) * HALF, sin_at:sin_at + LANE] = imag.astype(bf16)

                    mid = PLANES // 2
                    for z in range(mid + 1):
                        pc = plane_tab[h, z, 0, 2 * k + side:2 * k + side + 1, :]
                        ps = plane_tab[h, z, 1, 2 * k + side:2 * k + side + 1, :]
                        re_c, im_c = re * pc, im * pc
                        if z == 0:
                            put(mid, re_c, im_c)
                            continue
                        re_s, im_s = re * ps, im * ps
                        put(mid - z, re_c + im_s, im_c - re_s)
                        if z < mid:
                            put(mid + z, re_c - im_s, im_c + re_s)

    def third_copy(at, j):
        to = lax.rem(group + j, GROUPS)
        return pltpu.make_async_remote_copy(
            src_ref=send3.at[GROUPS * at + to], dst_ref=recv3.at[(GROUPS - 1) * at + j - 1], send_sem=s3.at[0],
            recv_sem=r3.at[at], device_id={"angle": to}, device_id_type=MESH)

    def planes(half):
        for tile in range(TILES):
            at = TILES * half + tile
            lanes = slice(TILE * tile, TILE * (tile + 1))
            z = dot_t(spread[half], back[lanes, :])
            own[...] = z
            for d in range(PLANES):
                send3[GROUPS * at + d] = z[d * HALF:(d + 1) * HALF, :].astype(bf16)

            def push(j, carry):
                third_copy(at, j).start()
                return carry

            lax.fori_loop(1, GROUPS, push, 0)
            out[0, half * HALF:(half + 1) * HALF, lanes] = own[pl.ds(pl.multiple_of(HALF * group, HALF), HALF), :]

    for half in range(HALVES):
        second_all(half).wait_recv()
        rytov(half)
        filtered(half)
        planes(half)

    for at in range(HALVES * TILES):
        first = (GROUPS - 1) * at
        pltpu.make_async_remote_copy(
            src_ref=send3.at[0:GROUPS - 1], dst_ref=recv3.at[first:first + GROUPS - 1], send_sem=s3.at[0],
            recv_sem=r3.at[at], device_id={"angle": group}, device_id_type=MESH).wait_recv()
        rows = slice(at // TILES * HALF, (at // TILES + 1) * HALF)
        lanes = slice(at % TILES * TILE, (at % TILES + 1) * TILE)
        total = out[0, rows, lanes]
        for j in range(GROUPS - 1):
            total = total + recv3[first + j].astype(f32)
        out[0, rows, lanes] = total

    first_all = pltpu.make_async_remote_copy(
        src_ref=send1.at[0:ROWS - 1], dst_ref=recv1.at[0:ROWS - 1], send_sem=s1.at[0], recv_sem=r1.at[0],
        device_id={"row": row}, device_id_type=MESH)
    first_all.wait_send()
    for half in range(HALVES):
        second_all(half).wait_send()
    count = HALVES * TILES * (GROUPS - 1)
    pltpu.make_async_remote_copy(
        src_ref=send3.at[0:count], dst_ref=recv3.at[0:count], send_sem=s3.at[0], recv_sem=r3.at[0],
        device_id={"angle": group}, device_id_type=MESH).wait_send()


def per_device(x_strip, y_strip, hologram, centres, offsets, angle_index):
    smem = pl.BlockSpec(memory_space=pltpu.SMEM)
    vmem = pl.BlockSpec(memory_space=pltpu.VMEM)
    anywhere = pl.BlockSpec(memory_space=pl.ANY)
    return pl.pallas_call(
        kernel,
        out_shape=pltpu.VMEM((1, SLAB, CROP), f32),
        in_specs=[smem, smem, smem, vmem, anywhere, anywhere],
        out_specs=vmem,
        scratch_shapes=[
            pltpu.VMEM(x_strip.shape, bf16),
            pltpu.VMEM(y_strip.shape, bf16),
            pltpu.VMEM((HELD, PIX // LANE, 2 * SLAB, LANE), f32),
            pltpu.VMEM((2 * HELD, PIX // LANE, LANE), f32),
            pltpu.VMEM((2 * HELD, SLAB, LANE), f32),
            pltpu.VMEM((2 * HELD * SLAB, PIX), bf16),
            pltpu.VMEM((2 * HELD * SLAB, PIX), bf16),
            pltpu.VMEM((2 * HELD, SLAB, CROP), f32),
            pltpu.VMEM((ROWS, SLAB, WIDE), bf16),
            pltpu.VMEM((ROWS, SLAB, WIDE), bf16),
            pltpu.VMEM((HALVES, ROWS, HALF, WIDE), bf16),
            pltpu.VMEM((HALVES, ROWS, HALF, WIDE), bf16),
            pltpu.VMEM((2, SLAB, CROP), f32),
            pltpu.VMEM((HALVES, 2 * HELD * HALF, CROP), bf16),
            pltpu.VMEM((CROP, 2 * CROP), bf16),
            pltpu.VMEM((CROP, 2 * HELD * CROP), bf16),
            pltpu.VMEM((2, CROP // 16, LANE), f32),
            pltpu.VMEM((HELD, PLANES // 2 + 1, 2, SLABS, LANE), f32),
            pltpu.VMEM((HALVES, PLANES * HALF, 2 * HELD * CROP), bf16),
            pltpu.VMEM((PLANES * HALF, TILE), f32),
            pltpu.VMEM((HALVES * TILES * GROUPS, HALF, TILE), bf16),
            pltpu.VMEM((HALVES * TILES * (GROUPS - 1), HALF, TILE), bf16),
            pltpu.SemaphoreType.DMA((2,)),
            pltpu.SemaphoreType.DMA((1,)),
            pltpu.SemaphoreType.DMA((1,)),
            pltpu.SemaphoreType.DMA((HALVES,)),
            pltpu.SemaphoreType.DMA((HALVES,)),
            pltpu.SemaphoreType.DMA((1,)),
            pltpu.SemaphoreType.DMA((HALVES * TILES,)),
        ],
        compiler_params=pltpu.CompilerParams(
            collective_id=0, has_side_effects=True, vmem_limit_bytes=56 * 1024 * 1024
        ),
    )(centres, angle_index, offsets, hologram, x_strip, y_strip)


def solution(mesh):
    x_strip, y_strip = half_band_strips()
    placed = (P("angle", "row", None), P("angle", None), P("angle", "row", None), P())
    return jax.shard_map(
        functools.partial(per_device, x_strip, y_strip),
        mesh=mesh, in_specs=placed, out_specs=P("angle", "row", None), check_vma=False
    )
```

```python
import functools
import math

import jax
import jax.numpy as jnp
import numpy as np
from jax import lax
from jax.experimental import pallas as pl
from jax.experimental.pallas import tpu as pltpu
from jax.sharding import PartitionSpec as P

PIX = 2048
CROP = 1024
BLOCK = 64
PLANES = 8
ANGLES = 1200
HOLOS = 16

ROWS = 16
GROUPS = 8
HELD = HOLOS // GROUPS
SLAB = CROP // ROWS
LANE = 128
WIDE = 256
SLABS = CROP // LANE
HALVES = 2
HALF = SLAB // HALVES
TILE = 512
TILES = CROP // TILE

MESH = pl.DeviceIdType.MESH
f32 = jnp.float32
bf16 = jnp.bfloat16

SIN = (6.283185302511503, -41.34170040531721, 81.6051313857832, -76.70301535364747, 42.02592698447418,
       -14.899846663536497, 3.2381375046186873)
COS = (0.9999999890590228, -19.73920449945383, 64.93911745989081, -85.45013953079767, 60.167630950263465,
       -25.967599245923743, 6.52865815775625)
ATAN = (0.9999999842426363, -0.33333066780691484, 0.19992483578502865, -0.14202570511730603, 0.10636754098309847,
        -0.07495445443851168, 0.04258760747298536, -0.016005030509000328, 0.002834064300549813)


def poly(coefs, v):
    total = jnp.full_like(v, coefs[-1])
    for coef in coefs[-2::-1]:
        total = total * v + f32(coef)
    return total


def turns(x):
    u = x - jnp.round(x)
    v = u * u
    return poly(COS, v), u * poly(SIN, v)


def half_band(n):
    n = n.astype(np.float64)
    with np.errstate(all="ignore"):
        odd = np.sin(np.pi * n / 2) / np.sin(np.pi * n / PIX) / CROP
    return np.where(n == 0, 1.0, np.where(n % 2 == 0, 0.0, odd))


def half_band_strips():
    x = np.arange(PIX + 3 * 512)[:, None] - 3 * 512
    b = np.arange(WIDE)
    along_x = half_band(2 * b[None, :] - x)
    i = np.arange(CROP + 3 * WIDE)[None, :] - 3 * WIDE
    b = b.reshape(4, HALVES, HALF).transpose(1, 0, 2).reshape(WIDE)
    along_y = half_band(2 * (b[:, None] - i) - 1)
    return along_x.astype(bf16), along_y.astype(bf16)


def iota(shape, dim):
    return lax.broadcasted_iota(jnp.int32, shape, dim)


def dot(a, b):
    return jnp.dot(a, b, preferred_element_type=f32)


def dot_t(a, b):
    return lax.dot_general(a, b, (((1,), (1,)), ((), ())), preferred_element_type=f32)


def kernel(centres, angle_index, offsets, hologram_hbm, x_hbm, y_hbm, out,
           hologram, x_strip, y_strip, raw, q_tab, p_tab, odd, evens, even, send1, recv1, send2, recv2, rot, ryt, wave, back,
           turn_tab, plane_tab, spread, own, send3, recv3, copy_sem, s1, r1, s2, r2, s3, r3):
    row = lax.axis_index("row")
    group = lax.axis_index("angle")

    barrier = pltpu.get_barrier_semaphore()
    h_copy = pltpu.make_async_copy(hologram_hbm, hologram, copy_sem.at[2])
    x_copy = pltpu.make_async_copy(x_hbm, x_strip, copy_sem.at[0])
    y_copy = pltpu.make_async_copy(y_hbm, y_strip, copy_sem.at[1])
    h_copy.start()
    x_copy.start()
    y_copy.start()

    def greet_row(i, carry):
        pl.semaphore_signal(barrier, inc=1, device_id={"row": lax.rem(row + i, ROWS)}, device_id_type=MESH)
        return carry

    def greet_group(i, carry):
        pl.semaphore_signal(barrier, inc=1, device_id={"angle": lax.rem(group + i, GROUPS)}, device_id_type=MESH)
        return carry

    lax.fori_loop(1, ROWS, greet_row, 0)
    lax.fori_loop(1, GROUPS, greet_group, 0)

    at_x = LANE * iota((PIX // LANE, LANE), 0) + iota((PIX // LANE, LANE), 1)
    for h in range(HELD):
        m = (at_x * (2 * centres[h, 0] - 1)) & (2 * PIX - 1)
        c, s = turns(m.astype(f32) * f32(1.0 / (2 * PIX)))
        q_tab[2 * h] = c
        q_tab[2 * h + 1] = -s
    at_y = 2 * SLAB * row + 2 * iota((SLAB, LANE), 0)

    def row_phases(parity):
        for h in range(HELD):
            m = ((at_y + (1 - parity)) * (2 * centres[h, 1] - 1)) & (2 * PIX - 1)
            c, s = turns(m.astype(f32) * f32(1.0 / (2 * PIX)))
            p_tab[2 * h] = 0.5 * c
            p_tab[2 * h + 1] = -0.5 * s

    def modulate(parity, to):
        for a in range(PIX // LANE):
            lanes = slice(a * LANE, (a + 1) * LANE)
            for h in range(HELD):
                if parity == 0:
                    raw[h, a] = hologram[h, :, lanes].astype(f32)
                block = raw[h, a, pl.ds(1 - parity, SLAB, stride=2), :]
                for part in range(2):
                    first = 2 * SLAB * h + SLAB * part
                    to[first:first + SLAB, lanes] = (block * q_tab[2 * h + part, a:a + 1, :]).astype(bf16)

    def across(source, block):
        weights = x_strip[pl.ds(pl.multiple_of(3 * 512 - 512 * block, 512), PIX), :]
        z = dot(source[...], weights)
        for h in range(HELD):
            for side in range(2):
                c = p_tab[2 * h]
                s = p_tab[2 * h + 1]
                re = z[2 * SLAB * h:2 * SLAB * h + SLAB, side * LANE:(side + 1) * LANE]
                im = z[2 * SLAB * h + SLAB:2 * SLAB * (h + 1), side * LANE:(side + 1) * LANE]
                yield h, side, re * c - im * s, re * s + im * c

    row_phases(0)
    h_copy.wait()
    modulate(0, odd)
    x_copy.wait()

    def first_copy(to):
        return pltpu.make_async_remote_copy(
            src_ref=send1.at[to], dst_ref=recv1.at[row], send_sem=s1.at[0], recv_sem=r1.at[0],
            device_id={"row": to}, device_id_type=MESH)

    for k in range(2):
        pair = lax.rem(row // 4 + k, 2)
        for half in range(2):
            block = 2 * pair + half
            for h, side, re, im in across(odd, block):
                to = SLABS * h + 2 * block + side
                send1[to, :, 0:LANE] = re.astype(bf16)
                send1[to, :, LANE:WIDE] = im.astype(bf16)

        if k == 0:
            pl.semaphore_wait(barrier, ROWS + GROUPS - 2)

        def push(i, carry):
            to = SLABS * (i // 4) + 4 * pair + lax.rem(row + i, 4)

            @pl.when(to != row)
            def _():
                first_copy(to).start()

            @pl.when(to == row)
            def _():
                recv1[row] = send1[row]
            return carry

        lax.fori_loop(0, 8, push, 0)

    def even_rows():
        modulate(1, evens)
        row_phases(1)
        for block in range(4):
            for h, side, re, im in across(evens, block):
                lanes = slice(WIDE * block + LANE * side, WIDE * block + LANE * (side + 1))
                even[2 * h, :, lanes] = re
                even[2 * h + 1, :, lanes] = im

    even_rows()

    def table(freq, target, cos_at):
        step = 16
        fine = iota((step, LANE), 0).astype(f32)
        coarse = ((iota((CROP // step, LANE), 0) - CROP // step // 2) * step).astype(f32)

        def columns(k, carry):
            def along(shape):
                return freq((iota(shape, 1) + (LANE * k - CROP // 2)).astype(f32))

            c0, s0 = turns(along((step, LANE)) * fine)
            c1, s1 = turns(along((CROP // step, LANE)) * coarse)
            turn_tab[0] = c1
            turn_tab[1] = s1
            cos_lanes = pl.ds(pl.multiple_of(cos_at + LANE * k, LANE), LANE)
            sin_lanes = pl.ds(pl.multiple_of(cos_at + CROP + LANE * k, LANE), LANE)
            for a in range(CROP // step):
                c = turn_tab[0, a:a + 1, :]
                s = turn_tab[1, a:a + 1, :]
                target[a * step:(a + 1) * step, cos_lanes] = (c0 * c - s0 * s).astype(bf16)
                target[a * step:(a + 1) * step, sin_lanes] = -(s0 * c + c0 * s).astype(bf16)
            return carry

        lax.fori_loop(0, SLABS, columns, 0)

    def tilt(h, shape):
        index = jnp.full(shape, angle_index[HELD * group + h], jnp.int32)
        return turns(index.astype(f32) * f32(1.0 / ANGLES))

    def axial(spatial):
        turn = spatial * f32(2.0 * math.pi)
        return (jnp.sqrt(16.0 - turn * turn) - 4.0) * f32(0.5 / math.pi)

    def back_table(h):
        def freq(j):
            c, s = tilt(h, j.shape)
            spatial = j * f32(1.0 / CROP)
            return spatial * c - axial(spatial) * s

        table(freq, back, 2 * h * CROP)

    table(lambda j: j * f32(1.0 / CROP), wave, 0)

    y_copy.wait()
    pltpu.make_async_remote_copy(
        src_ref=send1.at[0:ROWS - 1], dst_ref=recv1.at[0:ROWS - 1], send_sem=s1.at[0], recv_sem=r1.at[0],
        device_id={"row": row}, device_id_type=MESH).wait_recv()

    def second_copy(half, to):
        return pltpu.make_async_remote_copy(
            src_ref=send2.at[half, to], dst_ref=recv2.at[half, row], send_sem=s2.at[half], recv_sem=r2.at[half],
            device_id={"row": to}, device_id_type=MESH)

    def second_all(half):
        return pltpu.make_async_remote_copy(
            src_ref=send2.at[half, 0:ROWS - 1], dst_ref=recv2.at[half, 0:ROWS - 1], send_sem=s2.at[half],
            recv_sem=r2.at[half], device_id={"row": row}, device_id_type=MESH)

    gathered = recv1[...].reshape(CROP, WIDE)
    for half in range(HALVES):
        for block in range(4):
            first = 3 * WIDE - WIDE * block
            z = dot(y_strip[half * 4 * HALF:(half + 1) * 4 * HALF, first:first + CROP], gathered).astype(bf16)
            for part in range(4):
                send2[half, 4 * block + part] = z[HALF * part:HALF * (part + 1), :]

        def push(i, carry):
            second_copy(half, lax.rem(row + i, ROWS)).start()
            return carry

        lax.fori_loop(1, ROWS, push, 0)
        recv2[half, row] = send2[half, row]

    back_table(0)
    back_table(1)

    spatial = (LANE * iota((SLABS, LANE), 0) + iota((SLABS, LANE), 1) - CROP // 2).astype(f32) * f32(1.0 / CROP)
    ramp = jnp.abs(spatial) * f32(2.0 / math.sqrt(CROP * HOLOS) / math.sqrt(CROP))
    for h in range(HELD):
        c, s = tilt(h, (SLABS, LANE))
        beta = spatial * s + axial(spatial) * c
        for z in range(PLANES // 2 + 1):
            pc, ps = turns(beta * f32(z))
            plane_tab[h, z, 0] = pc * ramp
            plane_tab[h, z, 1] = ps * ramp

    def rotations(k, carry):
        at = LANE * k
        m = (iota((SLAB, LANE), 1) + at + iota((SLAB, LANE), 0) + SLAB * row).astype(f32)
        c, s = turns(m * f32(0.5 / CROP))
        lanes = pl.ds(pl.multiple_of(at, LANE), LANE)
        rot[0, :, lanes] = c
        rot[1, :, lanes] = -s
        return carry

    lax.fori_loop(0, SLABS, rotations, 0)

    left_half = iota((HALF, LANE), 1) < BLOCK

    def rytov(half):
        rows = slice(half * HALF, (half + 1) * HALF)

        def slab_of(slab, carry):
            lanes = pl.ds(pl.multiple_of(LANE * slab, LANE), LANE)
            c = rot[0, rows, lanes]
            s = rot[1, rows, lanes]
            for h in range(HELD):
                re = even[2 * h, rows, lanes] + recv2[half, SLABS * h + slab, :, 0:LANE].astype(f32)
                im = even[2 * h + 1, rows, lanes] + recv2[half, SLABS * h + slab, :, LANE:WIDE].astype(f32)
                field_re = re * c - im * s
                field_im = re * s + im * c
                energy = field_re * field_re + field_im * field_im + 1.0
                t = field_im / (jnp.sqrt(energy) + jnp.abs(field_re))
                unwrap = jnp.where(left_half, offsets[h, 0, 2 * slab], offsets[h, 0, 2 * slab + 1]).astype(f32)
                turned = 2.0 * (t * poly(ATAN, t * t)) + f32(2.0 * math.pi) * unwrap
                at = 2 * HALF * h
                ryt[half, at:at + HALF, lanes] = (0.5 * jnp.log(energy)).astype(bf16)
                ryt[half, at + HALF:at + 2 * HALF, lanes] = turned.astype(bf16)
            return carry

        lax.fori_loop(0, SLABS, slab_of, 0)

    def filtered(half):
        for k in range(CROP // WIDE):
            at = WIDE * k
            fc = dot(ryt[half], wave[:, at:at + WIDE])
            fs = dot(ryt[half], wave[:, CROP + at:CROP + at + WIDE])
            for h in range(HELD):
                top = slice(2 * HALF * h, 2 * HALF * h + HALF)
                low = slice(2 * HALF * h + HALF, 2 * HALF * (h + 1))
                for side in range(2):
                    lanes = slice(side * LANE, (side + 1) * LANE)
                    re = fc[top, lanes] - fs[low, lanes]
                    im = fc[low, lanes] + fs[top, lanes]
                    cos_at = 2 * CROP * h + at + side * LANE
                    sin_at = cos_at + CROP

                    def put(d, real, imag):
                        spread[half, d * HALF:(d + 1) * HALF, cos_at:cos_at + LANE] = real.astype(bf16)
                        spread[half, d * HALF:(d + 1) * HALF, sin_at:sin_at + LANE] = imag.astype(bf16)

                    mid = PLANES // 2
                    for z in range(mid + 1):
                        pc = plane_tab[h, z, 0, 2 * k + side:2 * k + side + 1, :]
                        ps = plane_tab[h, z, 1, 2 * k + side:2 * k + side + 1, :]
                        re_c, im_c = re * pc, im * pc
                        if z == 0:
                            put(mid, re_c, im_c)
                            continue
                        re_s, im_s = re * ps, im * ps
                        put(mid - z, re_c + im_s, im_c - re_s)
                        if z < mid:
                            put(mid + z, re_c - im_s, im_c + re_s)

    def third_copy(at, j):
        to = lax.rem(group + j, GROUPS)
        return pltpu.make_async_remote_copy(
            src_ref=send3.at[GROUPS * at + to], dst_ref=recv3.at[(GROUPS - 1) * at + j - 1], send_sem=s3.at[0],
            recv_sem=r3.at[at], device_id={"angle": to}, device_id_type=MESH)

    def planes(half):
        for tile in range(TILES):
            at = TILES * half + tile
            lanes = slice(TILE * tile, TILE * (tile + 1))
            z = dot_t(spread[half], back[lanes, :])
            own[...] = z
            for d in range(PLANES):
                send3[GROUPS * at + d] = z[d * HALF:(d + 1) * HALF, :].astype(bf16)

            def push(j, carry):
                third_copy(at, j).start()
                return carry

            lax.fori_loop(1, GROUPS, push, 0)
            out[0, half * HALF:(half + 1) * HALF, lanes] = own[pl.ds(pl.multiple_of(HALF * group, HALF), HALF), :]

    for half in range(HALVES):
        second_all(half).wait_recv()
        rytov(half)
        filtered(half)
        planes(half)

    for at in range(HALVES * TILES):
        first = (GROUPS - 1) * at
        pltpu.make_async_remote_copy(
            src_ref=send3.at[0:GROUPS - 1], dst_ref=recv3.at[first:first + GROUPS - 1], send_sem=s3.at[0],
            recv_sem=r3.at[at], device_id={"angle": group}, device_id_type=MESH).wait_recv()
        rows = slice(at // TILES * HALF, (at // TILES + 1) * HALF)
        lanes = slice(at % TILES * TILE, (at % TILES + 1) * TILE)
        total = out[0, rows, lanes]
        for j in range(GROUPS - 1):
            total = total + recv3[first + j].astype(f32)
        out[0, rows, lanes] = total

    first_all = pltpu.make_async_remote_copy(
        src_ref=send1.at[0:ROWS - 1], dst_ref=recv1.at[0:ROWS - 1], send_sem=s1.at[0], recv_sem=r1.at[0],
        device_id={"row": row}, device_id_type=MESH)
    first_all.wait_send()
    for half in range(HALVES):
        second_all(half).wait_send()
    count = HALVES * TILES * (GROUPS - 1)
    pltpu.make_async_remote_copy(
        src_ref=send3.at[0:count], dst_ref=recv3.at[0:count], send_sem=s3.at[0], recv_sem=r3.at[0],
        device_id={"angle": group}, device_id_type=MESH).wait_send()


def per_device(x_strip, y_strip, hologram, centres, offsets, angle_index):
    smem = pl.BlockSpec(memory_space=pltpu.SMEM)
    vmem = pl.BlockSpec(memory_space=pltpu.VMEM)
    anywhere = pl.BlockSpec(memory_space=pl.ANY)
    return pl.pallas_call(
        kernel,
        out_shape=pltpu.VMEM((1, SLAB, CROP), f32),
        in_specs=[smem, smem, smem, anywhere, anywhere, anywhere],
        out_specs=vmem,
        scratch_shapes=[
            pltpu.VMEM(hologram.shape, bf16),
            pltpu.VMEM(x_strip.shape, bf16),
            pltpu.VMEM(y_strip.shape, bf16),
            pltpu.VMEM((HELD, PIX // LANE, 2 * SLAB, LANE), f32),
            pltpu.VMEM((2 * HELD, PIX // LANE, LANE), f32),
            pltpu.VMEM((2 * HELD, SLAB, LANE), f32),
            pltpu.VMEM((2 * HELD * SLAB, PIX), bf16),
            pltpu.VMEM((2 * HELD * SLAB, PIX), bf16),
            pltpu.VMEM((2 * HELD, SLAB, CROP), f32),
            pltpu.VMEM((ROWS, SLAB, WIDE), bf16),
            pltpu.VMEM((ROWS, SLAB, WIDE), bf16),
            pltpu.VMEM((HALVES, ROWS, HALF, WIDE), bf16),
            pltpu.VMEM((HALVES, ROWS, HALF, WIDE), bf16),
            pltpu.VMEM((2, SLAB, CROP), f32),
            pltpu.VMEM((HALVES, 2 * HELD * HALF, CROP), bf16),
            pltpu.VMEM((CROP, 2 * CROP), bf16),
            pltpu.VMEM((CROP, 2 * HELD * CROP), bf16),
            pltpu.VMEM((2, CROP // 16, LANE), f32),
            pltpu.VMEM((HELD, PLANES // 2 + 1, 2, SLABS, LANE), f32),
            pltpu.VMEM((HALVES, PLANES * HALF, 2 * HELD * CROP), bf16),
            pltpu.VMEM((PLANES * HALF, TILE), f32),
            pltpu.VMEM((HALVES * TILES * GROUPS, HALF, TILE), bf16),
            pltpu.VMEM((HALVES * TILES * (GROUPS - 1), HALF, TILE), bf16),
            pltpu.SemaphoreType.DMA((3,)),
            pltpu.SemaphoreType.DMA((1,)),
            pltpu.SemaphoreType.DMA((1,)),
            pltpu.SemaphoreType.DMA((HALVES,)),
            pltpu.SemaphoreType.DMA((HALVES,)),
            pltpu.SemaphoreType.DMA((1,)),
            pltpu.SemaphoreType.DMA((HALVES * TILES,)),
        ],
        compiler_params=pltpu.CompilerParams(
            collective_id=0, has_side_effects=True, vmem_limit_bytes=56 * 1024 * 1024
        ),
    )(centres, angle_index, offsets, hologram, x_strip, y_strip)


def solution(mesh):
    x_strip, y_strip = half_band_strips()
    placed = (P("angle", "row", None), P("angle", None), P("angle", "row", None), P())
    return jax.shard_map(
        functools.partial(per_device, x_strip, y_strip),
        mesh=mesh, in_specs=placed, out_specs=P("angle", "row", None), check_vma=False
    )
```

```python
import functools
import math

import jax
import jax.numpy as jnp
import numpy as np
from jax import lax
from jax.experimental import pallas as pl
from jax.experimental.pallas import tpu as pltpu
from jax.sharding import PartitionSpec as P

PIX = 2048
CROP = 1024
BLOCK = 64
PLANES = 8
ANGLES = 1200
HOLOS = 16

ROWS = 16
GROUPS = 8
HELD = HOLOS // GROUPS
SLAB = CROP // ROWS
LANE = 128
WIDE = 256
SLABS = CROP // LANE
HALVES = 2
HALF = SLAB // HALVES
TILE = 512
TILES = CROP // TILE

MESH = pl.DeviceIdType.MESH
f32 = jnp.float32
bf16 = jnp.bfloat16

SIN = (6.283185302511503, -41.34170040531721, 81.6051313857832, -76.70301535364747, 42.02592698447418,
       -14.899846663536497, 3.2381375046186873)
COS = (0.9999999890590228, -19.73920449945383, 64.93911745989081, -85.45013953079767, 60.167630950263465,
       -25.967599245923743, 6.52865815775625)
ATAN = (0.9999999842426363, -0.33333066780691484, 0.19992483578502865, -0.14202570511730603, 0.10636754098309847,
        -0.07495445443851168, 0.04258760747298536, -0.016005030509000328, 0.002834064300549813)


def poly(coefs, v):
    total = jnp.full_like(v, coefs[-1])
    for coef in coefs[-2::-1]:
        total = total * v + f32(coef)
    return total


def turns(x):
    u = x - jnp.round(x)
    v = u * u
    return poly(COS, v), u * poly(SIN, v)


def half_band(n):
    n = n.astype(np.float64)
    with np.errstate(all="ignore"):
        odd = np.sin(np.pi * n / 2) / np.sin(np.pi * n / PIX) / CROP
    return np.where(n == 0, 1.0, np.where(n % 2 == 0, 0.0, odd))


def half_band_strips():
    x = np.arange(PIX + 3 * 512)[:, None] - 3 * 512
    b = np.arange(WIDE)
    along_x = half_band(2 * b[None, :] - x)
    i = np.arange(CROP + 3 * WIDE)[None, :] - 3 * WIDE
    b = b.reshape(4, HALVES, HALF).transpose(1, 0, 2).reshape(WIDE)
    along_y = half_band(2 * (b[:, None] - i) - 1)
    return along_x.astype(bf16), along_y.astype(bf16)


def iota(shape, dim):
    return lax.broadcasted_iota(jnp.int32, shape, dim)


def dot(a, b):
    return jnp.dot(a, b, preferred_element_type=f32)


def dot_t(a, b):
    return lax.dot_general(a, b, (((1,), (1,)), ((), ())), preferred_element_type=f32)


def kernel(centres_hbm, angle_hbm, offsets_hbm, hologram_hbm, x_hbm, y_hbm, out,
           centres, angle_index, offsets, hologram, x_strip, y_strip, raw, q_tab, p_tab, odd, evens, even, send1, recv1, send2, recv2, rot, ryt, wave, back,
           turn_tab, plane_tab, spread, own, send3, recv3, copy_sem, s1, r1, s2, r2, s3, r3):
    row = lax.axis_index("row")
    group = lax.axis_index("angle")

    barrier = pltpu.get_barrier_semaphore()
    h_copy = pltpu.make_async_copy(hologram_hbm, hologram, copy_sem.at[2])
    x_copy = pltpu.make_async_copy(x_hbm, x_strip, copy_sem.at[0])
    y_copy = pltpu.make_async_copy(y_hbm, y_strip, copy_sem.at[1])

    def greet_row(i, carry):
        pl.semaphore_signal(barrier, inc=1, device_id={"row": lax.rem(row + i, ROWS)}, device_id_type=MESH)
        return carry

    def greet_group(i, carry):
        pl.semaphore_signal(barrier, inc=1, device_id={"angle": lax.rem(group + i, GROUPS)}, device_id_type=MESH)
        return carry

    small = [
        pltpu.make_async_copy(centres_hbm, centres, copy_sem.at[3]),
        pltpu.make_async_copy(angle_hbm, angle_index, copy_sem.at[4]),
        pltpu.make_async_copy(offsets_hbm, offsets, copy_sem.at[5]),
    ]
    for copy in small:
        copy.start()
    h_copy.start()
    x_copy.start()
    lax.fori_loop(1, ROWS, greet_row, 0)
    lax.fori_loop(1, GROUPS, greet_group, 0)
    y_copy.start()
    for copy in small:
        copy.wait()

    at_x = LANE * iota((PIX // LANE, LANE), 0) + iota((PIX // LANE, LANE), 1)
    for h in range(HELD):
        m = (at_x * (2 * centres[h, 0] - 1)) & (2 * PIX - 1)
        c, s = turns(m.astype(f32) * f32(1.0 / (2 * PIX)))
        q_tab[2 * h] = c
        q_tab[2 * h + 1] = -s
    at_y = 2 * SLAB * row + 2 * iota((SLAB, LANE), 0)

    def row_phases(parity):
        for h in range(HELD):
            m = ((at_y + (1 - parity)) * (2 * centres[h, 1] - 1)) & (2 * PIX - 1)
            c, s = turns(m.astype(f32) * f32(1.0 / (2 * PIX)))
            p_tab[2 * h] = 0.5 * c
            p_tab[2 * h + 1] = -0.5 * s

    def modulate(parity, to):
        for a in range(PIX // LANE):
            lanes = slice(a * LANE, (a + 1) * LANE)
            for h in range(HELD):
                if parity == 0:
                    raw[h, a] = hologram[h, :, lanes].astype(f32)
                block = raw[h, a, pl.ds(1 - parity, SLAB, stride=2), :]
                for part in range(2):
                    first = 2 * SLAB * h + SLAB * part
                    to[first:first + SLAB, lanes] = (block * q_tab[2 * h + part, a:a + 1, :]).astype(bf16)

    def across(source, block):
        weights = x_strip[pl.ds(pl.multiple_of(3 * 512 - 512 * block, 512), PIX), :]
        z = dot(source[...], weights)
        for h in range(HELD):
            for side in range(2):
                c = p_tab[2 * h]
                s = p_tab[2 * h + 1]
                re = z[2 * SLAB * h:2 * SLAB * h + SLAB, side * LANE:(side + 1) * LANE]
                im = z[2 * SLAB * h + SLAB:2 * SLAB * (h + 1), side * LANE:(side + 1) * LANE]
                yield h, side, re * c - im * s, re * s + im * c

    row_phases(0)
    h_copy.wait()
    x_copy.wait()
    modulate(0, odd)

    def first_copy(part, to):
        return pltpu.make_async_remote_copy(
            src_ref=send1.at[part, to], dst_ref=recv1.at[part, row], send_sem=s1.at[part], recv_sem=r1.at[part],
            device_id={"row": to}, device_id_type=MESH)

    def first_all(part):
        return pltpu.make_async_remote_copy(
            src_ref=send1.at[part, 0:ROWS - 1], dst_ref=recv1.at[part, 0:ROWS - 1], send_sem=s1.at[part],
            recv_sem=r1.at[part], device_id={"row": row}, device_id_type=MESH)

    for block in range(4):
        for h, side, re, im in across(odd, block):
            to = SLABS * h + 2 * block + side
            send1[0, to] = re.astype(bf16)
            send1[1, to] = im.astype(bf16)

    pl.semaphore_wait(barrier, ROWS + GROUPS - 2)

    def push_real(i, carry):
        first_copy(0, lax.rem(row + i, ROWS)).start()
        return carry

    lax.fori_loop(1, ROWS, push_real, 0)

    def push_imag(i, carry):
        first_copy(1, lax.rem(row + i, ROWS)).start()
        return carry

    lax.fori_loop(1, ROWS, push_imag, 0)
    for part in range(2):
        recv1[part, row] = send1[part, row]

    def even_rows():
        modulate(1, evens)
        row_phases(1)
        for block in range(4):
            for h, side, re, im in across(evens, block):
                lanes = slice(WIDE * block + LANE * side, WIDE * block + LANE * (side + 1))
                even[2 * h, :, lanes] = re
                even[2 * h + 1, :, lanes] = im

    even_rows()

    def table(freq, target, cos_at):
        step = 16
        fine = iota((step, LANE), 0).astype(f32)
        coarse = ((iota((CROP // step, LANE), 0) - CROP // step // 2) * step).astype(f32)

        def columns(k, carry):
            def along(shape):
                return freq((iota(shape, 1) + (LANE * k - CROP // 2)).astype(f32))

            c0, s0 = turns(along((step, LANE)) * fine)
            c1, s1 = turns(along((CROP // step, LANE)) * coarse)
            turn_tab[0] = c1
            turn_tab[1] = s1
            cos_lanes = pl.ds(pl.multiple_of(cos_at + LANE * k, LANE), LANE)
            sin_lanes = pl.ds(pl.multiple_of(cos_at + CROP + LANE * k, LANE), LANE)
            for a in range(CROP // step):
                c = turn_tab[0, a:a + 1, :]
                s = turn_tab[1, a:a + 1, :]
                target[a * step:(a + 1) * step, cos_lanes] = (c0 * c - s0 * s).astype(bf16)
                target[a * step:(a + 1) * step, sin_lanes] = -(s0 * c + c0 * s).astype(bf16)
            return carry

        lax.fori_loop(0, SLABS, columns, 0)

    def tilt(h, shape):
        index = jnp.full(shape, angle_index[HELD * group + h], jnp.int32)
        return turns(index.astype(f32) * f32(1.0 / ANGLES))

    def axial(spatial):
        turn = spatial * f32(2.0 * math.pi)
        return (jnp.sqrt(16.0 - turn * turn) - 4.0) * f32(0.5 / math.pi)

    def back_table(h):
        def freq(j):
            c, s = tilt(h, j.shape)
            spatial = j * f32(1.0 / CROP)
            return spatial * c - axial(spatial) * s

        table(freq, back, 2 * h * CROP)

    table(lambda j: j * f32(1.0 / CROP), wave, 0)

    y_copy.wait()

    def second_copy(half, part, to):
        return pltpu.make_async_remote_copy(
            src_ref=send2.at[half, part, to], dst_ref=recv2.at[half, part, row], send_sem=s2.at[half, part],
            recv_sem=r2.at[half, part], device_id={"row": to}, device_id_type=MESH)

    def second_all(half, part):
        return pltpu.make_async_remote_copy(
            src_ref=send2.at[half, part, 0:ROWS - 1], dst_ref=recv2.at[half, part, 0:ROWS - 1],
            send_sem=s2.at[half, part], recv_sem=r2.at[half, part], device_id={"row": row}, device_id_type=MESH)

    def down(half, part):
        gathered = recv1[part].reshape(CROP, LANE)
        for block in range(4):
            first = 3 * WIDE - WIDE * block
            z = dot(y_strip[half * 4 * HALF:(half + 1) * 4 * HALF, first:first + CROP], gathered).astype(bf16)
            for slab in range(4):
                send2[half, part, 4 * block + slab] = z[HALF * slab:HALF * (slab + 1), :]

        def push(i, carry):
            second_copy(half, part, lax.rem(row + i, ROWS)).start()
            return carry

        lax.fori_loop(1, ROWS, push, 0)
        recv2[half, part, row] = send2[half, part, row]

    first_all(0).wait_recv()
    down(0, 0)
    first_all(1).wait_recv()
    down(0, 1)
    down(1, 0)
    down(1, 1)

    back_table(0)
    back_table(1)

    spatial = (LANE * iota((SLABS, LANE), 0) + iota((SLABS, LANE), 1) - CROP // 2).astype(f32) * f32(1.0 / CROP)
    ramp = jnp.abs(spatial) * f32(2.0 / math.sqrt(CROP * HOLOS) / math.sqrt(CROP))
    for h in range(HELD):
        c, s = tilt(h, (SLABS, LANE))
        beta = spatial * s + axial(spatial) * c
        for z in range(PLANES // 2 + 1):
            pc, ps = turns(beta * f32(z))
            plane_tab[h, z, 0] = pc * ramp
            plane_tab[h, z, 1] = ps * ramp

    def rotations(k, carry):
        at = LANE * k
        m = (iota((SLAB, LANE), 1) + at + iota((SLAB, LANE), 0) + SLAB * row).astype(f32)
        c, s = turns(m * f32(0.5 / CROP))
        lanes = pl.ds(pl.multiple_of(at, LANE), LANE)
        rot[0, :, lanes] = c
        rot[1, :, lanes] = -s
        return carry

    lax.fori_loop(0, SLABS, rotations, 0)

    left_half = iota((HALF, LANE), 1) < BLOCK

    def rytov(half):
        rows = slice(half * HALF, (half + 1) * HALF)

        def slab_of(slab, carry):
            lanes = pl.ds(pl.multiple_of(LANE * slab, LANE), LANE)
            c = rot[0, rows, lanes]
            s = rot[1, rows, lanes]
            for h in range(HELD):
                re = even[2 * h, rows, lanes] + recv2[half, 0, SLABS * h + slab].astype(f32)
                im = even[2 * h + 1, rows, lanes] + recv2[half, 1, SLABS * h + slab].astype(f32)
                field_re = re * c - im * s
                field_im = re * s + im * c
                energy = field_re * field_re + field_im * field_im + 1.0
                t = field_im / (jnp.sqrt(energy) + jnp.abs(field_re))
                unwrap = jnp.where(left_half, offsets[h, 0, 2 * slab], offsets[h, 0, 2 * slab + 1]).astype(f32)
                turned = 2.0 * (t * poly(ATAN, t * t)) + f32(2.0 * math.pi) * unwrap
                at = 2 * HALF * h
                ryt[half, at:at + HALF, lanes] = (0.5 * jnp.log(energy)).astype(bf16)
                ryt[half, at + HALF:at + 2 * HALF, lanes] = turned.astype(bf16)
            return carry

        lax.fori_loop(0, SLABS, slab_of, 0)

    def filtered(half):
        for k in range(CROP // WIDE):
            at = WIDE * k
            fc = dot(ryt[half], wave[:, at:at + WIDE])
            fs = dot(ryt[half], wave[:, CROP + at:CROP + at + WIDE])
            for h in range(HELD):
                top = slice(2 * HALF * h, 2 * HALF * h + HALF)
                low = slice(2 * HALF * h + HALF, 2 * HALF * (h + 1))
                for side in range(2):
                    lanes = slice(side * LANE, (side + 1) * LANE)
                    re = fc[top, lanes] - fs[low, lanes]
                    im = fc[low, lanes] + fs[top, lanes]
                    cos_at = 2 * CROP * h + at + side * LANE
                    sin_at = cos_at + CROP

                    def put(d, real, imag):
                        spread[half, d * HALF:(d + 1) * HALF, cos_at:cos_at + LANE] = real.astype(bf16)
                        spread[half, d * HALF:(d + 1) * HALF, sin_at:sin_at + LANE] = imag.astype(bf16)

                    mid = PLANES // 2
                    for z in range(mid + 1):
                        pc = plane_tab[h, z, 0, 2 * k + side:2 * k + side + 1, :]
                        ps = plane_tab[h, z, 1, 2 * k + side:2 * k + side + 1, :]
                        re_c, im_c = re * pc, im * pc
                        if z == 0:
                            put(mid, re_c, im_c)
                            continue
                        re_s, im_s = re * ps, im * ps
                        put(mid - z, re_c + im_s, im_c - re_s)
                        if z < mid:
                            put(mid + z, re_c - im_s, im_c + re_s)

    def third_copy(at, j):
        to = lax.rem(group + j, GROUPS)
        return pltpu.make_async_remote_copy(
            src_ref=send3.at[GROUPS * at + to], dst_ref=recv3.at[(GROUPS - 1) * at + j - 1], send_sem=s3.at[0],
            recv_sem=r3.at[at], device_id={"angle": to}, device_id_type=MESH)

    def planes(half):
        for tile in range(TILES):
            at = TILES * half + tile
            lanes = slice(TILE * tile, TILE * (tile + 1))
            z = dot_t(spread[half], back[lanes, :])
            own[...] = z
            for d in range(PLANES):
                send3[GROUPS * at + d] = z[d * HALF:(d + 1) * HALF, :].astype(bf16)

            def push(j, carry):
                third_copy(at, j).start()
                return carry

            lax.fori_loop(1, GROUPS, push, 0)
            out[0, half * HALF:(half + 1) * HALF, lanes] = own[pl.ds(pl.multiple_of(HALF * group, HALF), HALF), :]

    for half in range(HALVES):
        second_all(half, 0).wait_recv()
        second_all(half, 1).wait_recv()
        rytov(half)
        filtered(half)
        planes(half)

    for at in range(HALVES * TILES):
        first = (GROUPS - 1) * at
        pltpu.make_async_remote_copy(
            src_ref=send3.at[0:GROUPS - 1], dst_ref=recv3.at[first:first + GROUPS - 1], send_sem=s3.at[0],
            recv_sem=r3.at[at], device_id={"angle": group}, device_id_type=MESH).wait_recv()
        rows = slice(at // TILES * HALF, (at // TILES + 1) * HALF)
        lanes = slice(at % TILES * TILE, (at % TILES + 1) * TILE)
        total = out[0, rows, lanes]
        for j in range(GROUPS - 1):
            total = total + recv3[first + j].astype(f32)
        out[0, rows, lanes] = total

    for part in range(2):
        first_all(part).wait_send()
        for half in range(HALVES):
            second_all(half, part).wait_send()
    count = HALVES * TILES * (GROUPS - 1)
    pltpu.make_async_remote_copy(
        src_ref=send3.at[0:count], dst_ref=recv3.at[0:count], send_sem=s3.at[0], recv_sem=r3.at[0],
        device_id={"angle": group}, device_id_type=MESH).wait_send()


def per_device(x_strip, y_strip, hologram, centres, offsets, angle_index):
    vmem = pl.BlockSpec(memory_space=pltpu.VMEM)
    anywhere = pl.BlockSpec(memory_space=pl.ANY)
    return pl.pallas_call(
        kernel,
        out_shape=pltpu.VMEM((1, SLAB, CROP), f32),
        in_specs=[anywhere] * 6,
        out_specs=vmem,
        scratch_shapes=[
            pltpu.SMEM(centres.shape, jnp.int32),
            pltpu.SMEM(angle_index.shape, jnp.int32),
            pltpu.SMEM(offsets.shape, jnp.int32),
            pltpu.VMEM(hologram.shape, bf16),
            pltpu.VMEM(x_strip.shape, bf16),
            pltpu.VMEM(y_strip.shape, bf16),
            pltpu.VMEM((HELD, PIX // LANE, 2 * SLAB, LANE), f32),
            pltpu.VMEM((2 * HELD, PIX // LANE, LANE), f32),
            pltpu.VMEM((2 * HELD, SLAB, LANE), f32),
            pltpu.VMEM((2 * HELD * SLAB, PIX), bf16),
            pltpu.VMEM((2 * HELD * SLAB, PIX), bf16),
            pltpu.VMEM((2 * HELD, SLAB, CROP), f32),
            pltpu.VMEM((2, ROWS, SLAB, LANE), bf16),
            pltpu.VMEM((2, ROWS, SLAB, LANE), bf16),
            pltpu.VMEM((HALVES, 2, ROWS, HALF, LANE), bf16),
            pltpu.VMEM((HALVES, 2, ROWS, HALF, LANE), bf16),
            pltpu.VMEM((2, SLAB, CROP), f32),
            pltpu.VMEM((HALVES, 2 * HELD * HALF, CROP), bf16),
            pltpu.VMEM((CROP, 2 * CROP), bf16),
            pltpu.VMEM((CROP, 2 * HELD * CROP), bf16),
            pltpu.VMEM((2, CROP // 16, LANE), f32),
            pltpu.VMEM((HELD, PLANES // 2 + 1, 2, SLABS, LANE), f32),
            pltpu.VMEM((HALVES, PLANES * HALF, 2 * HELD * CROP), bf16),
            pltpu.VMEM((PLANES * HALF, TILE), f32),
            pltpu.VMEM((HALVES * TILES * GROUPS, HALF, TILE), bf16),
            pltpu.VMEM((HALVES * TILES * (GROUPS - 1), HALF, TILE), bf16),
            pltpu.SemaphoreType.DMA((6,)),
            pltpu.SemaphoreType.DMA((2,)),
            pltpu.SemaphoreType.DMA((2,)),
            pltpu.SemaphoreType.DMA((HALVES, 2)),
            pltpu.SemaphoreType.DMA((HALVES, 2)),
            pltpu.SemaphoreType.DMA((1,)),
            pltpu.SemaphoreType.DMA((HALVES * TILES,)),
        ],
        compiler_params=pltpu.CompilerParams(
            collective_id=0, has_side_effects=True, vmem_limit_bytes=56 * 1024 * 1024
        ),
    )(centres, angle_index, offsets, hologram, x_strip, y_strip)


def solution(mesh):
    x_strip, y_strip = half_band_strips()
    placed = (P("angle", "row", None), P("angle", None), P("angle", "row", None), P())
    return jax.shard_map(
        functools.partial(per_device, x_strip, y_strip),
        mesh=mesh, in_specs=placed, out_specs=P("angle", "row", None), check_vma=False
    )
```

```python
import functools
import math

import jax
import jax.numpy as jnp
import numpy as np
from jax import lax
from jax.experimental import pallas as pl
from jax.experimental.pallas import tpu as pltpu
from jax.sharding import PartitionSpec as P

PIX = 2048
CROP = 1024
BLOCK = 64
PLANES = 8
ANGLES = 1200
HOLOS = 16

ROWS = 16
GROUPS = 8
HELD = HOLOS // GROUPS
SLAB = CROP // ROWS
LANE = 128
WIDE = 256
SLABS = CROP // LANE
HALVES = 2
HALF = SLAB // HALVES
TILE = 512
TILES = CROP // TILE

MESH = pl.DeviceIdType.MESH
f32 = jnp.float32
bf16 = jnp.bfloat16

SIN = (6.283185302511503, -41.34170040531721, 81.6051313857832, -76.70301535364747, 42.02592698447418,
       -14.899846663536497, 3.2381375046186873)
COS = (0.9999999890590228, -19.73920449945383, 64.93911745989081, -85.45013953079767, 60.167630950263465,
       -25.967599245923743, 6.52865815775625)
ATAN = (0.9999999842426363, -0.33333066780691484, 0.19992483578502865, -0.14202570511730603, 0.10636754098309847,
        -0.07495445443851168, 0.04258760747298536, -0.016005030509000328, 0.002834064300549813)


def poly(coefs, v):
    total = jnp.full_like(v, coefs[-1])
    for coef in coefs[-2::-1]:
        total = total * v + f32(coef)
    return total


def turns(x):
    u = x - jnp.round(x)
    v = u * u
    return poly(COS, v), u * poly(SIN, v)


def half_band(n):
    n = n.astype(np.float64)
    with np.errstate(all="ignore"):
        odd = np.sin(np.pi * n / 2) / np.sin(np.pi * n / PIX) / CROP
    return np.where(n == 0, 1.0, np.where(n % 2 == 0, 0.0, odd))


def half_band_strips():
    x = np.arange(PIX + 3 * 512)[:, None] - 3 * 512
    b = np.arange(WIDE)
    along_x = half_band(2 * b[None, :] - x)
    i = np.arange(CROP + 3 * WIDE)[None, :] - 3 * WIDE
    b = b.reshape(4, HALVES, HALF).transpose(1, 0, 2).reshape(WIDE)
    along_y = half_band(2 * (b[:, None] - i) - 1)
    return along_x.astype(bf16), along_y.astype(bf16)


def iota(shape, dim):
    return lax.broadcasted_iota(jnp.int32, shape, dim)


def dot(a, b):
    return jnp.dot(a, b, preferred_element_type=f32)


def dot_t(a, b):
    return lax.dot_general(a, b, (((1,), (1,)), ((), ())), preferred_element_type=f32)


def kernel(centres_hbm, angle_hbm, offsets_hbm, hologram_hbm, x_hbm, y_hbm, out,
           centres, angle_index, offsets, hologram, x_strip, y_strip, raw, q_tab, p_tab, odd, evens, even, send1, recv1, send2, recv2, rot, ryt, wave, back,
           turn_tab, plane_tab, spread, own, send3, recv3, copy_sem, s1, r1, s2, r2, s3, r3):
    row = lax.axis_index("row")
    group = lax.axis_index("angle")

    barrier = pltpu.get_barrier_semaphore()
    h_copy = pltpu.make_async_copy(hologram_hbm, hologram, copy_sem.at[2])
    x_copy = pltpu.make_async_copy(x_hbm, x_strip, copy_sem.at[0])
    y_copy = pltpu.make_async_copy(y_hbm, y_strip, copy_sem.at[1])

    def greet_row(i, carry):
        pl.semaphore_signal(barrier, inc=1, device_id={"row": lax.rem(row + i, ROWS)}, device_id_type=MESH)
        return carry

    def greet_group(i, carry):
        pl.semaphore_signal(barrier, inc=1, device_id={"angle": lax.rem(group + i, GROUPS)}, device_id_type=MESH)
        return carry

    small = [
        pltpu.make_async_copy(centres_hbm, centres, copy_sem.at[3]),
        pltpu.make_async_copy(angle_hbm, angle_index, copy_sem.at[4]),
        pltpu.make_async_copy(offsets_hbm, offsets, copy_sem.at[5]),
    ]
    for copy in small:
        copy.start()
    h_copy.start()
    x_copy.start()
    lax.fori_loop(1, ROWS, greet_row, 0)
    lax.fori_loop(1, GROUPS, greet_group, 0)
    y_copy.start()
    for copy in small:
        copy.wait()

    at_x = LANE * iota((PIX // LANE, LANE), 0) + iota((PIX // LANE, LANE), 1)
    for h in range(HELD):
        m = (at_x * (2 * centres[h, 0] - 1)) & (2 * PIX - 1)
        c, s = turns(m.astype(f32) * f32(1.0 / (2 * PIX)))
        q_tab[2 * h] = c
        q_tab[2 * h + 1] = -s
    at_y = 2 * SLAB * row + 2 * iota((SLAB, LANE), 0)

    def row_phases(parity):
        for h in range(HELD):
            m = ((at_y + (1 - parity)) * (2 * centres[h, 1] - 1)) & (2 * PIX - 1)
            c, s = turns(m.astype(f32) * f32(1.0 / (2 * PIX)))
            p_tab[2 * h] = 0.5 * c
            p_tab[2 * h + 1] = -0.5 * s

    def modulate(parity, to):
        for a in range(PIX // LANE):
            lanes = slice(a * LANE, (a + 1) * LANE)
            for h in range(HELD):
                if parity == 0:
                    raw[h, a] = hologram[h, :, lanes].astype(f32)
                block = raw[h, a, pl.ds(1 - parity, SLAB, stride=2), :]
                for part in range(2):
                    first = 2 * SLAB * h + SLAB * part
                    to[first:first + SLAB, lanes] = (block * q_tab[2 * h + part, a:a + 1, :]).astype(bf16)

    def across(source, block):
        weights = x_strip[pl.ds(pl.multiple_of(3 * 512 - 512 * block, 512), PIX), :]
        z = dot(source[...], weights)
        for h in range(HELD):
            for side in range(2):
                c = p_tab[2 * h]
                s = p_tab[2 * h + 1]
                re = z[2 * SLAB * h:2 * SLAB * h + SLAB, side * LANE:(side + 1) * LANE]
                im = z[2 * SLAB * h + SLAB:2 * SLAB * (h + 1), side * LANE:(side + 1) * LANE]
                yield h, side, re * c - im * s, re * s + im * c

    row_phases(0)
    h_copy.wait()
    x_copy.wait()
    modulate(0, odd)

    def first_copy(part, to):
        return pltpu.make_async_remote_copy(
            src_ref=send1.at[part, to], dst_ref=recv1.at[part, row], send_sem=s1.at[part], recv_sem=r1.at[part],
            device_id={"row": to}, device_id_type=MESH)

    def first_all(part):
        return pltpu.make_async_remote_copy(
            src_ref=send1.at[part, 0:ROWS - 1], dst_ref=recv1.at[part, 0:ROWS - 1], send_sem=s1.at[part],
            recv_sem=r1.at[part], device_id={"row": row}, device_id_type=MESH)

    for block in range(4):
        for h, side, re, im in across(odd, block):
            to = SLABS * h + 2 * block + side
            send1[0, to] = re.astype(bf16)
            send1[1, to] = im.astype(bf16)

    pl.semaphore_wait(barrier, ROWS + GROUPS - 2)

    def push_real(i, carry):
        first_copy(0, lax.rem(row + i, ROWS)).start()
        return carry

    lax.fori_loop(1, ROWS, push_real, 0)

    def push_imag(i, carry):
        first_copy(1, lax.rem(row + i, ROWS)).start()
        return carry

    lax.fori_loop(1, ROWS, push_imag, 0)
    for part in range(2):
        recv1[part, row] = send1[part, row]

    def even_rows():
        modulate(1, evens)
        row_phases(1)
        for block in range(4):
            for h, side, re, im in across(evens, block):
                lanes = slice(WIDE * block + LANE * side, WIDE * block + LANE * (side + 1))
                even[2 * h, :, lanes] = re
                even[2 * h + 1, :, lanes] = im

    even_rows()

    def table(freq, target, cos_at):
        step = 16
        fine = iota((step, LANE), 0).astype(f32)
        coarse = ((iota((CROP // step, LANE), 0) - CROP // step // 2) * step).astype(f32)

        def columns(k, carry):
            def along(shape):
                return freq((iota(shape, 1) + (LANE * k - CROP // 2)).astype(f32))

            c0, s0 = turns(along((step, LANE)) * fine)
            c1, s1 = turns(along((CROP // step, LANE)) * coarse)
            turn_tab[0] = c1
            turn_tab[1] = s1
            cos_lanes = pl.ds(pl.multiple_of(cos_at + LANE * k, LANE), LANE)
            sin_lanes = pl.ds(pl.multiple_of(cos_at + CROP + LANE * k, LANE), LANE)
            for a in range(CROP // step):
                c = turn_tab[0, a:a + 1, :]
                s = turn_tab[1, a:a + 1, :]
                target[a * step:(a + 1) * step, cos_lanes] = (c0 * c - s0 * s).astype(bf16)
                target[a * step:(a + 1) * step, sin_lanes] = -(s0 * c + c0 * s).astype(bf16)
            return carry

        lax.fori_loop(0, SLABS, columns, 0)

    def tilt(h, shape):
        index = jnp.full(shape, angle_index[HELD * group + h], jnp.int32)
        return turns(index.astype(f32) * f32(1.0 / ANGLES))

    def axial(spatial):
        turn = spatial * f32(2.0 * math.pi)
        return (jnp.sqrt(16.0 - turn * turn) - 4.0) * f32(0.5 / math.pi)

    def back_table(h):
        def freq(j):
            c, s = tilt(h, j.shape)
            spatial = j * f32(1.0 / CROP)
            return spatial * c - axial(spatial) * s

        table(freq, back, 2 * h * CROP)

    table(lambda j: j * f32(1.0 / CROP), wave, 0)

    spatial = (LANE * iota((SLABS, LANE), 0) + iota((SLABS, LANE), 1) - CROP // 2).astype(f32) * f32(1.0 / CROP)
    ramp = jnp.abs(spatial) * f32(2.0 / math.sqrt(CROP * HOLOS) / math.sqrt(CROP))
    for h in range(HELD):
        c, s = tilt(h, (SLABS, LANE))
        beta = spatial * s + axial(spatial) * c
        for z in range(PLANES // 2 + 1):
            pc, ps = turns(beta * f32(z))
            plane_tab[h, z, 0] = pc * ramp
            plane_tab[h, z, 1] = ps * ramp

    def rotations(k, carry):
        at = LANE * k
        m = (iota((SLAB, LANE), 1) + at + iota((SLAB, LANE), 0) + SLAB * row).astype(f32)
        c, s = turns(m * f32(0.5 / CROP))
        lanes = pl.ds(pl.multiple_of(at, LANE), LANE)
        rot[0, :, lanes] = c
        rot[1, :, lanes] = -s
        return carry

    lax.fori_loop(0, SLABS, rotations, 0)

    y_copy.wait()

    def second_copy(half, part, to):
        return pltpu.make_async_remote_copy(
            src_ref=send2.at[half, part, to], dst_ref=recv2.at[half, part, row], send_sem=s2.at[half, part],
            recv_sem=r2.at[half, part], device_id={"row": to}, device_id_type=MESH)

    def second_all(half, part):
        return pltpu.make_async_remote_copy(
            src_ref=send2.at[half, part, 0:ROWS - 1], dst_ref=recv2.at[half, part, 0:ROWS - 1],
            send_sem=s2.at[half, part], recv_sem=r2.at[half, part], device_id={"row": row}, device_id_type=MESH)

    def down(half, part):
        gathered = recv1[part].reshape(CROP, LANE)
        for block in range(4):
            first = 3 * WIDE - WIDE * block
            z = dot(y_strip[half * 4 * HALF:(half + 1) * 4 * HALF, first:first + CROP], gathered).astype(bf16)
            for slab in range(4):
                send2[half, part, 4 * block + slab] = z[HALF * slab:HALF * (slab + 1), :]

        recv2[half, part, row] = send2[half, part, row]

    def push_second(half, part):
        def push(i, carry):
            second_copy(half, part, lax.rem(row + i, ROWS)).start()
            return carry

        lax.fori_loop(1, ROWS, push, 0)

    back_table(0)
    first_all(0).wait_recv()
    down(0, 0)
    push_second(0, 0)
    down(1, 0)
    first_all(1).wait_recv()
    down(0, 1)
    push_second(0, 1)
    push_second(1, 0)
    down(1, 1)
    push_second(1, 1)
    back_table(1)

    left_half = iota((HALF, LANE), 1) < BLOCK

    def rytov(half):
        rows = slice(half * HALF, (half + 1) * HALF)

        def slab_of(slab, carry):
            lanes = pl.ds(pl.multiple_of(LANE * slab, LANE), LANE)
            c = rot[0, rows, lanes]
            s = rot[1, rows, lanes]
            for h in range(HELD):
                re = even[2 * h, rows, lanes] + recv2[half, 0, SLABS * h + slab].astype(f32)
                im = even[2 * h + 1, rows, lanes] + recv2[half, 1, SLABS * h + slab].astype(f32)
                field_re = re * c - im * s
                field_im = re * s + im * c
                energy = field_re * field_re + field_im * field_im + 1.0
                t = field_im / (jnp.sqrt(energy) + jnp.abs(field_re))
                unwrap = jnp.where(left_half, offsets[h, 0, 2 * slab], offsets[h, 0, 2 * slab + 1]).astype(f32)
                turned = 2.0 * (t * poly(ATAN, t * t)) + f32(2.0 * math.pi) * unwrap
                at = 2 * HALF * h
                ryt[half, at:at + HALF, lanes] = (0.5 * jnp.log(energy)).astype(bf16)
                ryt[half, at + HALF:at + 2 * HALF, lanes] = turned.astype(bf16)
            return carry

        lax.fori_loop(0, SLABS, slab_of, 0, unroll=4)

    def filtered(half):
        for k in range(CROP // WIDE):
            at = WIDE * k
            fc = dot(ryt[half], wave[:, at:at + WIDE])
            fs = dot(ryt[half], wave[:, CROP + at:CROP + at + WIDE])
            for h in range(HELD):
                top = slice(2 * HALF * h, 2 * HALF * h + HALF)
                low = slice(2 * HALF * h + HALF, 2 * HALF * (h + 1))
                for side in range(2):
                    lanes = slice(side * LANE, (side + 1) * LANE)
                    re = fc[top, lanes] - fs[low, lanes]
                    im = fc[low, lanes] + fs[top, lanes]
                    cos_at = 2 * CROP * h + at + side * LANE
                    sin_at = cos_at + CROP

                    def put(d, real, imag):
                        spread[half, d * HALF:(d + 1) * HALF, cos_at:cos_at + LANE] = real.astype(bf16)
                        spread[half, d * HALF:(d + 1) * HALF, sin_at:sin_at + LANE] = imag.astype(bf16)

                    mid = PLANES // 2
                    for z in range(mid + 1):
                        pc = plane_tab[h, z, 0, 2 * k + side:2 * k + side + 1, :]
                        ps = plane_tab[h, z, 1, 2 * k + side:2 * k + side + 1, :]
                        re_c, im_c = re * pc, im * pc
                        if z == 0:
                            put(mid, re_c, im_c)
                            continue
                        re_s, im_s = re * ps, im * ps
                        put(mid - z, re_c + im_s, im_c - re_s)
                        if z < mid:
                            put(mid + z, re_c - im_s, im_c + re_s)

    def third_copy(at, j):
        to = lax.rem(group + j, GROUPS)
        return pltpu.make_async_remote_copy(
            src_ref=send3.at[GROUPS * at + to], dst_ref=recv3.at[(GROUPS - 1) * at + j - 1], send_sem=s3.at[0],
            recv_sem=r3.at[at], device_id={"angle": to}, device_id_type=MESH)

    def planes(half):
        for tile in range(TILES):
            at = TILES * half + tile
            lanes = slice(TILE * tile, TILE * (tile + 1))
            z = dot_t(spread[half], back[lanes, :])
            own[...] = z
            for d in range(PLANES):
                send3[GROUPS * at + d] = z[d * HALF:(d + 1) * HALF, :].astype(bf16)

            def push(j, carry):
                third_copy(at, j).start()
                return carry

            lax.fori_loop(1, GROUPS, push, 0)
            out[0, half * HALF:(half + 1) * HALF, lanes] = own[pl.ds(pl.multiple_of(HALF * group, HALF), HALF), :]

    for half in range(HALVES):
        second_all(half, 0).wait_recv()
        second_all(half, 1).wait_recv()
        rytov(half)
        filtered(half)
        planes(half)

    for at in range(HALVES * TILES):
        first = (GROUPS - 1) * at
        pltpu.make_async_remote_copy(
            src_ref=send3.at[0:GROUPS - 1], dst_ref=recv3.at[first:first + GROUPS - 1], send_sem=s3.at[0],
            recv_sem=r3.at[at], device_id={"angle": group}, device_id_type=MESH).wait_recv()
        rows = slice(at // TILES * HALF, (at // TILES + 1) * HALF)
        lanes = slice(at % TILES * TILE, (at % TILES + 1) * TILE)
        total = out[0, rows, lanes]
        for j in range(GROUPS - 1):
            total = total + recv3[first + j].astype(f32)
        out[0, rows, lanes] = total

    for part in range(2):
        first_all(part).wait_send()
        for half in range(HALVES):
            second_all(half, part).wait_send()
    count = HALVES * TILES * (GROUPS - 1)
    pltpu.make_async_remote_copy(
        src_ref=send3.at[0:count], dst_ref=recv3.at[0:count], send_sem=s3.at[0], recv_sem=r3.at[0],
        device_id={"angle": group}, device_id_type=MESH).wait_send()


def per_device(x_strip, y_strip, hologram, centres, offsets, angle_index):
    vmem = pl.BlockSpec(memory_space=pltpu.VMEM)
    anywhere = pl.BlockSpec(memory_space=pl.ANY)
    return pl.pallas_call(
        kernel,
        out_shape=pltpu.VMEM((1, SLAB, CROP), f32),
        in_specs=[anywhere] * 6,
        out_specs=vmem,
        scratch_shapes=[
            pltpu.SMEM(centres.shape, jnp.int32),
            pltpu.SMEM(angle_index.shape, jnp.int32),
            pltpu.SMEM(offsets.shape, jnp.int32),
            pltpu.VMEM(hologram.shape, bf16),
            pltpu.VMEM(x_strip.shape, bf16),
            pltpu.VMEM(y_strip.shape, bf16),
            pltpu.VMEM((HELD, PIX // LANE, 2 * SLAB, LANE), f32),
            pltpu.VMEM((2 * HELD, PIX // LANE, LANE), f32),
            pltpu.VMEM((2 * HELD, SLAB, LANE), f32),
            pltpu.VMEM((2 * HELD * SLAB, PIX), bf16),
            pltpu.VMEM((2 * HELD * SLAB, PIX), bf16),
            pltpu.VMEM((2 * HELD, SLAB, CROP), f32),
            pltpu.VMEM((2, ROWS, SLAB, LANE), bf16),
            pltpu.VMEM((2, ROWS, SLAB, LANE), bf16),
            pltpu.VMEM((HALVES, 2, ROWS, HALF, LANE), bf16),
            pltpu.VMEM((HALVES, 2, ROWS, HALF, LANE), bf16),
            pltpu.VMEM((2, SLAB, CROP), f32),
            pltpu.VMEM((HALVES, 2 * HELD * HALF, CROP), bf16),
            pltpu.VMEM((CROP, 2 * CROP), bf16),
            pltpu.VMEM((CROP, 2 * HELD * CROP), bf16),
            pltpu.VMEM((2, CROP // 16, LANE), f32),
            pltpu.VMEM((HELD, PLANES // 2 + 1, 2, SLABS, LANE), f32),
            pltpu.VMEM((HALVES, PLANES * HALF, 2 * HELD * CROP), bf16),
            pltpu.VMEM((PLANES * HALF, TILE), f32),
            pltpu.VMEM((HALVES * TILES * GROUPS, HALF, TILE), bf16),
            pltpu.VMEM((HALVES * TILES * (GROUPS - 1), HALF, TILE), bf16),
            pltpu.SemaphoreType.DMA((6,)),
            pltpu.SemaphoreType.DMA((2,)),
            pltpu.SemaphoreType.DMA((2,)),
            pltpu.SemaphoreType.DMA((HALVES, 2)),
            pltpu.SemaphoreType.DMA((HALVES, 2)),
            pltpu.SemaphoreType.DMA((1,)),
            pltpu.SemaphoreType.DMA((HALVES * TILES,)),
        ],
        compiler_params=pltpu.CompilerParams(
            collective_id=0, has_side_effects=True, vmem_limit_bytes=56 * 1024 * 1024
        ),
    )(centres, angle_index, offsets, hologram, x_strip, y_strip)


def solution(mesh):
    x_strip, y_strip = half_band_strips()
    placed = (P("angle", "row", None), P("angle", None), P("angle", "row", None), P())
    return jax.shard_map(
        functools.partial(per_device, x_strip, y_strip),
        mesh=mesh, in_specs=placed, out_specs=P("angle", "row", None), check_vma=False
    )
```

```python
import functools
import math

import jax
import jax.numpy as jnp
import numpy as np
from jax import lax
from jax.experimental import pallas as pl
from jax.experimental.pallas import tpu as pltpu
from jax.sharding import PartitionSpec as P

PIX = 2048
CROP = 1024
BLOCK = 64
PLANES = 8
ANGLES = 1200
HOLOS = 16

ROWS = 16
GROUPS = 8
HELD = HOLOS // GROUPS
SLAB = CROP // ROWS
LANE = 128
WIDE = 256
SLABS = CROP // LANE
HALVES = 2
HALF = SLAB // HALVES
TILE = 512
TILES = CROP // TILE

MESH = pl.DeviceIdType.MESH
f32 = jnp.float32
bf16 = jnp.bfloat16

SIN = (6.283185302511503, -41.34170040531721, 81.6051313857832, -76.70301535364747, 42.02592698447418,
       -14.899846663536497, 3.2381375046186873)
COS = (0.9999999890590228, -19.73920449945383, 64.93911745989081, -85.45013953079767, 60.167630950263465,
       -25.967599245923743, 6.52865815775625)
ATAN = (0.9999999842426363, -0.33333066780691484, 0.19992483578502865, -0.14202570511730603, 0.10636754098309847,
        -0.07495445443851168, 0.04258760747298536, -0.016005030509000328, 0.002834064300549813)


def poly(coefs, v):
    total = jnp.full_like(v, coefs[-1])
    for coef in coefs[-2::-1]:
        total = total * v + f32(coef)
    return total


def turns(x):
    u = x - jnp.round(x)
    v = u * u
    return poly(COS, v), u * poly(SIN, v)


def half_band(n):
    n = n.astype(np.float64)
    with np.errstate(all="ignore"):
        odd = np.sin(np.pi * n / 2) / np.sin(np.pi * n / PIX) / CROP
    return np.where(n == 0, 1.0, np.where(n % 2 == 0, 0.0, odd))


def half_band_strips():
    x = np.arange(PIX + 3 * 512)[:, None] - 3 * 512
    b = np.arange(WIDE)
    along_x = half_band(2 * b[None, :] - x)
    i = np.arange(CROP + 3 * WIDE)[None, :] - 3 * WIDE
    b = b.reshape(4, HALVES, HALF).transpose(1, 0, 2).reshape(WIDE)
    along_y = half_band(2 * (b[:, None] - i) - 1)
    return along_x.astype(bf16), along_y.astype(bf16)


def iota(shape, dim):
    return lax.broadcasted_iota(jnp.int32, shape, dim)


def dot(a, b):
    return jnp.dot(a, b, preferred_element_type=f32)


def dot_t(a, b):
    return lax.dot_general(a, b, (((1,), (1,)), ((), ())), preferred_element_type=f32)


def kernel(centres_hbm, angle_hbm, offsets_hbm, hologram_hbm, x_hbm, y_hbm, out,
           centres, angle_index, offsets, hologram, x_strip, y_strip, raw, q_tab, p_tab, odd, evens, even, send1, recv1, send2, recv2, rot, ryt, wave, back,
           turn_tab, plane_tab, spread, own, send3, recv3, copy_sem, s1, r1, s2, r2, s3, r3):
    row = lax.axis_index("row")
    group = lax.axis_index("angle")

    barrier = pltpu.get_barrier_semaphore()
    h_copy = pltpu.make_async_copy(hologram_hbm, hologram, copy_sem.at[2])
    x_copy = pltpu.make_async_copy(x_hbm, x_strip, copy_sem.at[0])
    y_copy = pltpu.make_async_copy(y_hbm, y_strip, copy_sem.at[1])

    def greet_row(i, carry):
        pl.semaphore_signal(barrier, inc=1, device_id={"row": lax.rem(row + i, ROWS)}, device_id_type=MESH)
        return carry

    def greet_group(i, carry):
        pl.semaphore_signal(barrier, inc=1, device_id={"angle": lax.rem(group + i, GROUPS)}, device_id_type=MESH)
        return carry

    small = [
        pltpu.make_async_copy(centres_hbm, centres, copy_sem.at[3]),
        pltpu.make_async_copy(angle_hbm, angle_index, copy_sem.at[4]),
        pltpu.make_async_copy(offsets_hbm, offsets, copy_sem.at[5]),
    ]
    h_copy.start()
    lax.fori_loop(1, ROWS, greet_row, 0, unroll=True)
    lax.fori_loop(1, GROUPS, greet_group, 0, unroll=True)
    for copy in small:
        copy.start()
    x_copy.start()
    y_copy.start()
    for copy in small:
        copy.wait()

    at_x = LANE * iota((PIX // LANE, LANE), 0) + iota((PIX // LANE, LANE), 1)
    for h in range(HELD):
        m = (at_x * (2 * centres[h, 0] - 1)) & (2 * PIX - 1)
        c, s = turns(m.astype(f32) * f32(1.0 / (2 * PIX)))
        q_tab[2 * h] = c
        q_tab[2 * h + 1] = -s
    at_y = 2 * SLAB * row + 2 * iota((SLAB, LANE), 0)

    def row_phases(parity):
        for h in range(HELD):
            m = ((at_y + (1 - parity)) * (2 * centres[h, 1] - 1)) & (2 * PIX - 1)
            c, s = turns(m.astype(f32) * f32(1.0 / (2 * PIX)))
            p_tab[2 * h] = 0.5 * c
            p_tab[2 * h + 1] = -0.5 * s

    def modulate(parity, to):
        for a in range(PIX // LANE):
            lanes = slice(a * LANE, (a + 1) * LANE)
            for h in range(HELD):
                if parity == 0:
                    raw[h, a] = hologram[h, :, lanes].astype(f32)
                block = raw[h, a, pl.ds(1 - parity, SLAB, stride=2), :]
                for part in range(2):
                    first = 2 * SLAB * h + SLAB * part
                    to[first:first + SLAB, lanes] = (block * q_tab[2 * h + part, a:a + 1, :]).astype(bf16)

    def across(source, block):
        weights = x_strip[pl.ds(pl.multiple_of(3 * 512 - 512 * block, 512), PIX), :]
        z = dot(source[...], weights)
        for h in range(HELD):
            for side in range(2):
                c = p_tab[2 * h]
                s = p_tab[2 * h + 1]
                re = z[2 * SLAB * h:2 * SLAB * h + SLAB, side * LANE:(side + 1) * LANE]
                im = z[2 * SLAB * h + SLAB:2 * SLAB * (h + 1), side * LANE:(side + 1) * LANE]
                yield h, side, re * c - im * s, re * s + im * c

    row_phases(0)
    h_copy.wait()
    x_copy.wait()
    modulate(0, odd)

    def first_copy(part, to):
        return pltpu.make_async_remote_copy(
            src_ref=send1.at[part, to], dst_ref=recv1.at[part, row], send_sem=s1.at[part], recv_sem=r1.at[part],
            device_id={"row": to}, device_id_type=MESH)

    def first_all(part):
        return pltpu.make_async_remote_copy(
            src_ref=send1.at[part, 0:ROWS - 1], dst_ref=recv1.at[part, 0:ROWS - 1], send_sem=s1.at[part],
            recv_sem=r1.at[part], device_id={"row": row}, device_id_type=MESH)

    for block in range(4):
        for h, side, re, im in across(odd, block):
            to = SLABS * h + 2 * block + side
            send1[0, to] = re.astype(bf16)
            send1[1, to] = im.astype(bf16)

    pl.semaphore_wait(barrier, ROWS + GROUPS - 2)

    def push_real(i, carry):
        first_copy(0, lax.rem(row + i, ROWS)).start()
        return carry

    lax.fori_loop(1, ROWS, push_real, 0)

    def push_imag(i, carry):
        first_copy(1, lax.rem(row + i, ROWS)).start()
        return carry

    lax.fori_loop(1, ROWS, push_imag, 0)
    for part in range(2):
        recv1[part, row] = send1[part, row]

    def even_rows():
        modulate(1, evens)
        row_phases(1)
        for block in range(4):
            for h, side, re, im in across(evens, block):
                lanes = slice(WIDE * block + LANE * side, WIDE * block + LANE * (side + 1))
                even[2 * h, :, lanes] = re
                even[2 * h + 1, :, lanes] = im

    even_rows()

    def table(freq, target, cos_at):
        step = 16
        fine = iota((step, LANE), 0).astype(f32)
        coarse = ((iota((CROP // step, LANE), 0) - CROP // step // 2) * step).astype(f32)

        def columns(k, carry):
            def along(shape):
                return freq((iota(shape, 1) + (LANE * k - CROP // 2)).astype(f32))

            c0, s0 = turns(along((step, LANE)) * fine)
            c1, s1 = turns(along((CROP // step, LANE)) * coarse)
            turn_tab[0] = c1
            turn_tab[1] = s1
            cos_lanes = pl.ds(pl.multiple_of(cos_at + LANE * k, LANE), LANE)
            sin_lanes = pl.ds(pl.multiple_of(cos_at + CROP + LANE * k, LANE), LANE)
            for a in range(CROP // step):
                c = turn_tab[0, a:a + 1, :]
                s = turn_tab[1, a:a + 1, :]
                target[a * step:(a + 1) * step, cos_lanes] = (c0 * c - s0 * s).astype(bf16)
                target[a * step:(a + 1) * step, sin_lanes] = -(s0 * c + c0 * s).astype(bf16)
            return carry

        lax.fori_loop(0, SLABS, columns, 0)

    def tilt(h, shape):
        index = jnp.full(shape, angle_index[HELD * group + h], jnp.int32)
        return turns(index.astype(f32) * f32(1.0 / ANGLES))

    def axial(spatial):
        turn = spatial * f32(2.0 * math.pi)
        return (jnp.sqrt(16.0 - turn * turn) - 4.0) * f32(0.5 / math.pi)

    def back_table(h):
        def freq(j):
            c, s = tilt(h, j.shape)
            spatial = j * f32(1.0 / CROP)
            return spatial * c - axial(spatial) * s

        table(freq, back, 2 * h * CROP)

    table(lambda j: j * f32(1.0 / CROP), wave, 0)

    spatial = (LANE * iota((SLABS, LANE), 0) + iota((SLABS, LANE), 1) - CROP // 2).astype(f32) * f32(1.0 / CROP)
    ramp = jnp.abs(spatial) * f32(2.0 / math.sqrt(CROP * HOLOS) / math.sqrt(CROP))
    for h in range(HELD):
        c, s = tilt(h, (SLABS, LANE))
        beta = spatial * s + axial(spatial) * c
        for z in range(PLANES // 2 + 1):
            pc, ps = turns(beta * f32(z))
            plane_tab[h, z, 0] = pc * ramp
            plane_tab[h, z, 1] = ps * ramp

    def rotations(k, carry):
        at = LANE * k
        m = (iota((SLAB, LANE), 1) + at + iota((SLAB, LANE), 0) + SLAB * row).astype(f32)
        c, s = turns(m * f32(0.5 / CROP))
        lanes = pl.ds(pl.multiple_of(at, LANE), LANE)
        rot[0, :, lanes] = c
        rot[1, :, lanes] = -s
        return carry

    lax.fori_loop(0, SLABS, rotations, 0)

    y_copy.wait()

    def second_copy(half, part, to):
        return pltpu.make_async_remote_copy(
            src_ref=send2.at[half, part, to], dst_ref=recv2.at[half, part, row], send_sem=s2.at[half, part],
            recv_sem=r2.at[half, part], device_id={"row": to}, device_id_type=MESH)

    def second_all(half, part):
        return pltpu.make_async_remote_copy(
            src_ref=send2.at[half, part, 0:ROWS - 1], dst_ref=recv2.at[half, part, 0:ROWS - 1],
            send_sem=s2.at[half, part], recv_sem=r2.at[half, part], device_id={"row": row}, device_id_type=MESH)

    def down(half, part):
        gathered = recv1[part].reshape(CROP, LANE)
        for block in range(4):
            first = 3 * WIDE - WIDE * block
            z = dot(y_strip[half * 4 * HALF:(half + 1) * 4 * HALF, first:first + CROP], gathered).astype(bf16)
            for slab in range(4):
                send2[half, part, 4 * block + slab] = z[HALF * slab:HALF * (slab + 1), :]

        recv2[half, part, row] = send2[half, part, row]

    def push_second(half, part):
        def push(i, carry):
            second_copy(half, part, lax.rem(row + i, ROWS)).start()
            return carry

        lax.fori_loop(1, ROWS, push, 0)

    back_table(0)
    first_all(0).wait_recv()
    down(0, 0)
    push_second(0, 0)
    down(1, 0)
    first_all(1).wait_recv()
    down(0, 1)
    push_second(0, 1)
    push_second(1, 0)
    down(1, 1)
    push_second(1, 1)
    back_table(1)

    left_half = iota((HALF, LANE), 1) < BLOCK

    def rytov(half):
        rows = slice(half * HALF, (half + 1) * HALF)

        def slab_of(slab, carry):
            lanes = pl.ds(pl.multiple_of(LANE * slab, LANE), LANE)
            c = rot[0, rows, lanes]
            s = rot[1, rows, lanes]
            for h in range(HELD):
                re = even[2 * h, rows, lanes] + recv2[half, 0, SLABS * h + slab].astype(f32)
                im = even[2 * h + 1, rows, lanes] + recv2[half, 1, SLABS * h + slab].astype(f32)
                field_re = re * c - im * s
                field_im = re * s + im * c
                energy = field_re * field_re + field_im * field_im + 1.0
                t = field_im / (jnp.sqrt(energy) + jnp.abs(field_re))
                unwrap = jnp.where(left_half, offsets[h, 0, 2 * slab], offsets[h, 0, 2 * slab + 1]).astype(f32)
                turned = 2.0 * (t * poly(ATAN, t * t)) + f32(2.0 * math.pi) * unwrap
                at = 2 * HALF * h
                ryt[half, at:at + HALF, lanes] = (0.5 * jnp.log(energy)).astype(bf16)
                ryt[half, at + HALF:at + 2 * HALF, lanes] = turned.astype(bf16)
            return carry

        lax.fori_loop(0, SLABS, slab_of, 0, unroll=4)

    def filtered(half):
        for k in range(CROP // WIDE):
            at = WIDE * k
            fc = dot(ryt[half], wave[:, at:at + WIDE])
            fs = dot(ryt[half], wave[:, CROP + at:CROP + at + WIDE])
            for h in range(HELD):
                top = slice(2 * HALF * h, 2 * HALF * h + HALF)
                low = slice(2 * HALF * h + HALF, 2 * HALF * (h + 1))
                for side in range(2):
                    lanes = slice(side * LANE, (side + 1) * LANE)
                    re = fc[top, lanes] - fs[low, lanes]
                    im = fc[low, lanes] + fs[top, lanes]
                    cos_at = 2 * CROP * h + at + side * LANE
                    sin_at = cos_at + CROP

                    def put(d, real, imag):
                        spread[half, d * HALF:(d + 1) * HALF, cos_at:cos_at + LANE] = real.astype(bf16)
                        spread[half, d * HALF:(d + 1) * HALF, sin_at:sin_at + LANE] = imag.astype(bf16)

                    mid = PLANES // 2
                    for z in range(mid + 1):
                        pc = plane_tab[h, z, 0, 2 * k + side:2 * k + side + 1, :]
                        ps = plane_tab[h, z, 1, 2 * k + side:2 * k + side + 1, :]
                        re_c, im_c = re * pc, im * pc
                        if z == 0:
                            put(mid, re_c, im_c)
                            continue
                        re_s, im_s = re * ps, im * ps
                        put(mid - z, re_c + im_s, im_c - re_s)
                        if z < mid:
                            put(mid + z, re_c - im_s, im_c + re_s)

    def third_copy(at, j):
        to = lax.rem(group + j, GROUPS)
        return pltpu.make_async_remote_copy(
            src_ref=send3.at[GROUPS * at + to], dst_ref=recv3.at[(GROUPS - 1) * at + j - 1], send_sem=s3.at[0],
            recv_sem=r3.at[at], device_id={"angle": to}, device_id_type=MESH)

    def planes(half):
        for tile in range(TILES):
            at = TILES * half + tile
            lanes = slice(TILE * tile, TILE * (tile + 1))
            z = dot_t(spread[half], back[lanes, :])
            own[...] = z
            for d in range(PLANES):
                send3[GROUPS * at + d] = z[d * HALF:(d + 1) * HALF, :].astype(bf16)

            def push(j, carry):
                third_copy(at, j).start()
                return carry

            lax.fori_loop(1, GROUPS, push, 0)
            out[0, half * HALF:(half + 1) * HALF, lanes] = own[pl.ds(pl.multiple_of(HALF * group, HALF), HALF), :]

    for half in range(HALVES):
        second_all(half, 0).wait_recv()
        second_all(half, 1).wait_recv()
        rytov(half)
        filtered(half)
        planes(half)

    for at in range(HALVES * TILES):
        first = (GROUPS - 1) * at
        pltpu.make_async_remote_copy(
            src_ref=send3.at[0:GROUPS - 1], dst_ref=recv3.at[first:first + GROUPS - 1], send_sem=s3.at[0],
            recv_sem=r3.at[at], device_id={"angle": group}, device_id_type=MESH).wait_recv()
        rows = slice(at // TILES * HALF, (at // TILES + 1) * HALF)
        lanes = slice(at % TILES * TILE, (at % TILES + 1) * TILE)
        total = out[0, rows, lanes]
        for j in range(GROUPS - 1):
            total = total + recv3[first + j].astype(f32)
        out[0, rows, lanes] = total

    for part in range(2):
        first_all(part).wait_send()
        for half in range(HALVES):
            second_all(half, part).wait_send()
    count = HALVES * TILES * (GROUPS - 1)
    pltpu.make_async_remote_copy(
        src_ref=send3.at[0:count], dst_ref=recv3.at[0:count], send_sem=s3.at[0], recv_sem=r3.at[0],
        device_id={"angle": group}, device_id_type=MESH).wait_send()


def per_device(x_strip, y_strip, hologram, centres, offsets, angle_index):
    vmem = pl.BlockSpec(memory_space=pltpu.VMEM)
    anywhere = pl.BlockSpec(memory_space=pl.ANY)
    return pl.pallas_call(
        kernel,
        out_shape=pltpu.VMEM((1, SLAB, CROP), f32),
        in_specs=[anywhere] * 6,
        out_specs=vmem,
        scratch_shapes=[
            pltpu.SMEM(centres.shape, jnp.int32),
            pltpu.SMEM(angle_index.shape, jnp.int32),
            pltpu.SMEM(offsets.shape, jnp.int32),
            pltpu.VMEM(hologram.shape, bf16),
            pltpu.VMEM(x_strip.shape, bf16),
            pltpu.VMEM(y_strip.shape, bf16),
            pltpu.VMEM((HELD, PIX // LANE, 2 * SLAB, LANE), f32),
            pltpu.VMEM((2 * HELD, PIX // LANE, LANE), f32),
            pltpu.VMEM((2 * HELD, SLAB, LANE), f32),
            pltpu.VMEM((2 * HELD * SLAB, PIX), bf16),
            pltpu.VMEM((2 * HELD * SLAB, PIX), bf16),
            pltpu.VMEM((2 * HELD, SLAB, CROP), f32),
            pltpu.VMEM((2, ROWS, SLAB, LANE), bf16),
            pltpu.VMEM((2, ROWS, SLAB, LANE), bf16),
            pltpu.VMEM((HALVES, 2, ROWS, HALF, LANE), bf16),
            pltpu.VMEM((HALVES, 2, ROWS, HALF, LANE), bf16),
            pltpu.VMEM((2, SLAB, CROP), f32),
            pltpu.VMEM((HALVES, 2 * HELD * HALF, CROP), bf16),
            pltpu.VMEM((CROP, 2 * CROP), bf16),
            pltpu.VMEM((CROP, 2 * HELD * CROP), bf16),
            pltpu.VMEM((2, CROP // 16, LANE), f32),
            pltpu.VMEM((HELD, PLANES // 2 + 1, 2, SLABS, LANE), f32),
            pltpu.VMEM((HALVES, PLANES * HALF, 2 * HELD * CROP), bf16),
            pltpu.VMEM((PLANES * HALF, TILE), f32),
            pltpu.VMEM((HALVES * TILES * GROUPS, HALF, TILE), bf16),
            pltpu.VMEM((HALVES * TILES * (GROUPS - 1), HALF, TILE), bf16),
            pltpu.SemaphoreType.DMA((6,)),
            pltpu.SemaphoreType.DMA((2,)),
            pltpu.SemaphoreType.DMA((2,)),
            pltpu.SemaphoreType.DMA((HALVES, 2)),
            pltpu.SemaphoreType.DMA((HALVES, 2)),
            pltpu.SemaphoreType.DMA((1,)),
            pltpu.SemaphoreType.DMA((HALVES * TILES,)),
        ],
        compiler_params=pltpu.CompilerParams(
            collective_id=0, has_side_effects=True, vmem_limit_bytes=56 * 1024 * 1024
        ),
    )(centres, angle_index, offsets, hologram, x_strip, y_strip)


def solution(mesh):
    x_strip, y_strip = half_band_strips()
    placed = (P("angle", "row", None), P("angle", None), P("angle", "row", None), P())
    return jax.shard_map(
        functools.partial(per_device, x_strip, y_strip),
        mesh=mesh, in_specs=placed, out_specs=P("angle", "row", None), check_vma=False
    )
```
